128 devices in a mesh: dp: 32 (over x, y, core), psg: 4 (over z).
Axes of the slice: x: 4, y: 4, z: 4, core: 2. Of those that a mesh axis runs over, the one named last changes fastest.
Arguments:
- query_states: bfloat16 [4096, 4096], P('dp'), may hold values from -6 to 6
- passage_last_states: bfloat16 [65536, 4096], P(('dp', 'psg')), may hold values from -6 to 6
- head_weight: bfloat16 [4096, 2048], P(None, 'psg'), may hold values from -0.09375 to 0.09375
- negatives: int32 [4, 512, 2], P(None, 'dp'), may hold values from 0 to 31, all different within a row; in each aligned block of 16 rows (0 to 15, 16 to 31, ..., all dimensions but the last counted through in order) at most 2 rows name the same one
- positives: int32 [4096], P('dp'), may hold values from 0 to 511
Outputs:
- losses: float32 [4096], P(('dp', 'psg'))
- grad_weight: bfloat16 [4096, 2048], P(None, 'psg')
The draws below stay inside these ranges and needn't reach their ends.
Inputs may be any that keep to these rules, and one draw needn't show every extreme that they name: `negatives`: for each c and each aligned group of 16 query blocks (those of one dp index), no dp index appears more than 2 times among their column-c entries, and some reaches 2; the 2 entries of one row differ.
All inputs are finite; a program needn't handle non-finite values.
Results may differ from the reference program's by a relative error of at most 0.012.
Values may be sent and summed in bfloat16 or wider, within the bound.
No kernel may reach another device: no remote copies, remote signals or barrier semaphores. Data moves between devices by JAX's collectives and lax.ppermute only.
A program may use at most 128 MiB of HBM per device.

```python
import math
import jax
import jax.numpy as jnp
import numpy as np
from jax import lax

D = 4096
E = 2048
QPB = 8
PBLK = 512
QBK_DEV = 16
SLOTS = 2
CAP = 2
NQB = 512
NQ = 4096
NP = 65536
N_DP = 32
N_PSG = 4


def set_ends(result, stream_key, smallest, high):
    index_at = [jax.random.randint(jax.random.fold_in(stream_key, axis), (), 0, length) for axis, length in enumerate(result.shape)]
    main_axis = result.shape.index(max(result.shape))
    next_to = index_at[:main_axis] + [(index_at[main_axis] + 1) % result.shape[main_axis]] + index_at[main_axis + 1:]
    return result.at[tuple(index_at)].set(smallest).at[tuple(next_to)].set(high)


def shard_levels(stream_key, dims, split, smallest, high):
    factor_of, own = 1.0, jax.random.fold_in(stream_key, 6)
    for position, blocks in split:
        draws = jnp.exp(jax.random.uniform(jax.random.fold_in(own, position), (blocks,), jnp.float32, smallest / len(split), high / len(split)))
        factor_of = factor_of * jnp.repeat(draws, dims[position] // blocks).reshape([-1 if axis == position else 1 for axis in range(len(dims))])
    return factor_of


def deal_out(rng, own, number, rows, amount, top, most, lean):
    sequence = jax.random.permutation(rng, amount)
    heavy_load, common = portions_of(amount, rows * top, most, lean, True), portions_of(amount, rows * top, most, lean, False)
    places = jnp.arange(amount)

    def named(sizes, turn):
        used = int((sizes > 0).sum())
        fixed = max(1, used // 4)
        passed = fixed + (places - fixed + turn * (used - fixed)) % max(1, amount - fixed)
        return jnp.zeros((amount,), jnp.int32).at[sequence[jnp.where(places < fixed, places, passed)]].set(jnp.asarray(sizes, jnp.int32))

    sizes = jnp.where(number % 4 == 0, named(heavy_load, number // 4), named(common, number - number // 4 - 1))
    mixed = jax.random.permutation(jax.random.fold_in(own, 3), amount)
    giver, taker = mixed[0:amount // 2 * 2:2], mixed[1:amount // 2 * 2:2]
    room = jnp.minimum(sizes[giver] - 1, most - sizes[taker]) // 2
    room = jnp.where((giver == sequence[0]) | (taker == sequence[0]) | (sizes[taker] == 0), 0, jnp.maximum(room, 0))
    passed = jax.random.randint(jax.random.fold_in(own, 4), (amount // 2,), 0, 1 << 20) % (room + 1)
    sizes = sizes.at[giver].add(-passed).at[taker].add(passed)
    items = jnp.searchsorted(jnp.cumsum(sizes), jnp.arange(rows * top), side="right").astype(jnp.int32)
    table = items.reshape(top, rows).T
    table = table[jax.random.permutation(jax.random.fold_in(own, 1), rows)]
    turn = jax.random.randint(jax.random.fold_in(own, 2), (rows, 1), 0, top)
    return jnp.take_along_axis(table, (jnp.arange(top)[None, :] + turn) % top, axis=1)


def portions_of(amount, total, most, skew, full):
    loads = [(1 << 20) // math.isqrt(rank ** skew) + 1 for rank in range(1, amount + 1)]
    largest = most if full else min(most, max(-(-total // amount), total * loads[0] // sum(loads)))
    least = 1 if total - largest >= amount - 1 else 0
    holding, rest = [largest] + [least] * (amount - 1), total - largest - least * (amount - 1)
    while rest > 0:
        free = [i for i in range(1, amount) if holding[i] < largest] or [i for i in range(1, amount) if holding[i] < most]
        whole, left = sum([loads[i] for i in free]), rest
        for i in free:
            more = min(most - holding[i], max(1, left * loads[i] // whole), rest)
            holding[i] = holding[i] + more
            rest = rest - more
    return np.array(holding)


def gaussian(own_key, dims, width, reach, split=(), kind=jnp.bfloat16):
    entries = jax.random.normal(own_key, dims, jnp.float32) * width
    if len(split) > 0:
        entries = shard_levels(own_key, dims, split, -0.22, 0.18) * entries
    return jnp.clip(entries, min=-reach, max=reach).astype(kind)


def setup_inputs(seed: int = 0) -> dict:
    keys = jax.random.split(jax.random.key(seed), 6)
    query_states = gaussian(keys[0], (NQ, D), 1.0, 6.0, ((0, 32),))
    passage_last_states = gaussian(keys[1], (NP, D), 1.0, 6.0, ((0, 128),))
    head_weight = gaussian(keys[2], (D, E), D ** -0.5, 0.09375, ((1, 4),))
    negatives_keys = jax.random.split(jax.random.fold_in(keys[3], 1), N_PSG * NQB // QBK_DEV)
    negatives_turns = jax.random.permutation(jax.random.fold_in(keys[3], 3), N_PSG * NQB // QBK_DEV)
    negatives = jax.vmap(lambda own, number: deal_out(jax.random.fold_in(keys[3], 2), own, number, QBK_DEV, N_DP, SLOTS, CAP, 2))(negatives_keys, negatives_turns).reshape((N_PSG, NQB, SLOTS))
    positives = set_ends(jax.random.randint(keys[4], (NQ,), 0, PBLK), jax.random.fold_in(keys[4], 1), 0, PBLK - 1).astype(jnp.int32)
    return {"query_states": query_states, "passage_last_states": passage_last_states, "head_weight": head_weight, "negatives": negatives, "positives": positives}


INV_TAU = 50.0

def embed(states, weight):
    raw = jnp.dot(states, weight, preferred_element_type=jnp.float32)
    scale = 1.0 / jnp.sqrt(lax.optimization_barrier(jnp.sum(raw * raw, axis=1, keepdims=True)) + 1e-06)
    return (raw * scale, scale)

def backward_norm(unit, scale, d_emb):
    inner = lax.optimization_barrier(jnp.sum(unit * d_emb, axis=1, keepdims=True))
    return ((d_emb - unit * inner) * scale).astype(jnp.bfloat16)

def reference(query_states, passage_last_states, head_weight, negatives, positives):
    unit_q, scale_q = embed(query_states, head_weight)
    unit_p, scale_p = embed(passage_last_states, head_weight)
    emb_q = unit_q.astype(jnp.bfloat16)
    emb_p = unit_p.astype(jnp.bfloat16)
    passage_blocks = emb_p.reshape(NP // PBLK, PBLK, E)
    columns = jnp.arange(N_PSG, dtype=jnp.int32)[:, None, None]
    block_ids = jnp.transpose(negatives * N_PSG + columns, (1, 0, 2)).reshape(NQB, N_PSG * SLOTS).astype(jnp.int32)
    query_block_list = emb_q.reshape(NQB, QPB, E)
    chosen = positives.reshape(NQB, QPB)
    first = jnp.arange(N_PSG * SLOTS, dtype=jnp.int32) == 0

    def step(d_emb_p, inputs):
        queries, ids, picks = inputs
        candidates = passage_blocks[ids].astype(jnp.float32)
        scores = jnp.einsum('qd,knd->qkn', queries.astype(jnp.float32), candidates) * INV_TAU
        logsum = jnp.log(lax.optimization_barrier(jnp.sum(jnp.exp(scores), axis=(1, 2))))
        target = (first[None, :, None] & (jnp.arange(PBLK, dtype=jnp.int32)[None, None, :] == picks[:, None, None])).astype(jnp.float32)
        positive = lax.optimization_barrier(jnp.sum(scores * target, axis=(1, 2)))
        grads = (jnp.exp(scores - logsum[:, None, None]) - target).astype(jnp.bfloat16)
        terms = (jnp.einsum('qkn,knd->qkd', grads.astype(jnp.float32), candidates) * INV_TAU).astype(jnp.bfloat16)
        d_query = lax.optimization_barrier(jnp.sum(terms.astype(jnp.float32), axis=1))
        d_cand = jnp.einsum('qkn,qd->knd', grads.astype(jnp.float32), queries.astype(jnp.float32)) * INV_TAU
        d_emb_p = d_emb_p.at[ids].add(d_cand)
        return (d_emb_p, (logsum - positive, d_query))
    start = jnp.zeros((NP // PBLK, PBLK, E), jnp.float32)
    d_emb_p, (losses, d_emb_q) = lax.scan(step, start, (query_block_list, block_ids, chosen))
    d_raw_q = backward_norm(unit_q, scale_q, d_emb_q.reshape(NQ, E))
    d_raw_p = backward_norm(unit_p, scale_p, d_emb_p.reshape(NP, E))
    grad = jnp.dot(query_states.T, d_raw_q, preferred_element_type=jnp.float32)
    grad = grad + jnp.dot(passage_last_states.T, d_raw_p, preferred_element_type=jnp.float32)
    return (losses.reshape(NQ), grad.astype(jnp.bfloat16))
```

```python
import jax
import jax.numpy as jnp
from jax import lax
from jax.sharding import PartitionSpec as P

CAP = 2
INV_TAU = 50.0
F32 = jnp.float32
BF16 = jnp.bfloat16
SIDE = 4


def dp_perm(move):
    pairs = []
    for x in range(SIDE):
        for y in range(SIDE):
            for core in range(2):
                tx, ty, tcore = move(x, y, core)
                target = ((tx % SIDE) * SIDE + ty % SIDE) * 2 + tcore
                pairs.append(((x * SIDE + y) * 2 + core, target))
    return pairs


def first(value, step):
    return lax.ppermute(
        value, "dp", dp_perm(lambda x, y, k: (x + step, y, k) if k == 0 else (x, y + step, k))
    )


def second(value, step):
    return lax.ppermute(
        value, "dp", dp_perm(lambda x, y, k: (x, y + step, k) if k == 0 else (x + step, y, k))
    )


def third(value, step):
    return lax.ppermute(value, "psg", [(c, (c + step) % SIDE) for c in range(SIDE)])


def swap(value):
    return lax.ppermute(value, "dp", dp_perm(lambda x, y, k: (x, y, 1 - k)))


def ring_scatter(chunk, move):
    far = chunk(2)
    half = far.shape[0] // 2
    from_left = move(far[:half], 1)
    from_right = move(far[half:], -1)
    right = chunk(1)
    left = chunk(3)
    right = jnp.concatenate(
        [(right[:half].astype(F32) + from_left.astype(F32)).astype(BF16), right[half:]], axis=0
    )
    left = jnp.concatenate(
        [left[:half], (left[half:].astype(F32) + from_right.astype(F32)).astype(BF16)], axis=0
    )
    from_left = move(right, 1)
    from_right = move(left, -1)
    own = chunk(0)
    return own.astype(F32) + from_left.astype(F32) + from_right.astype(F32)


def ring_gather(piece, move, place):
    half = piece.shape[0] // 2
    left = move(piece, 1)
    right = move(piece, -1)
    far = jnp.concatenate([move(left[:half], 1), move(right[half:], -1)], axis=0)
    rows = piece.shape[0]
    out = jnp.concatenate([piece, right, far, left] * 2, axis=0)
    start = lax.rem(SIDE - place, SIDE) * rows
    return lax.dynamic_slice_in_dim(out, start, SIDE * rows, 0)


def ring_sum(value, move):
    return value + move(value, 1) + move(value, -1) + move(value, 2)


def project(states, pieces):
    return [jnp.dot(states, piece, preferred_element_type=F32) for piece in pieces]


def routes(mine, per_block, ranks):
    blocks, slots = mine.shape
    same = (mine[:, :, None, None] == mine[None, None, :, :]).astype(jnp.int32)
    before = (
        lax.broadcasted_iota(jnp.int32, (blocks, blocks), 1)
        < lax.broadcasted_iota(jnp.int32, (blocks, blocks), 0)
    ).astype(jnp.int32)
    place = jnp.sum(same * before[:, None, :, None], axis=(2, 3))
    line = mine * CAP + place
    rows = ranks * CAP * per_block
    line = jnp.repeat(line, per_block, axis=0)
    count = blocks * per_block
    row = lax.broadcasted_iota(jnp.int32, (rows, count), 0)
    col = lax.broadcasted_iota(jnp.int32, (rows, count), 1)
    aligned = lax.rem(row, per_block) == lax.rem(col, per_block)
    row_line = row // per_block
    hot = [aligned & (row_line == line[None, :, s]) for s in range(slots)]
    return (hot[0] | hot[1]).astype(BF16), hot[0].astype(BF16)


def shards(query_states, passage_last_states, head_weight, negatives, positives):
    ranks = lax.axis_size("dp")
    groups = lax.axis_size("psg")
    dp = lax.axis_index("dp")
    column = lax.axis_index("psg")
    core = lax.rem(dp, 2)
    x = dp // (2 * SIDE)
    y = lax.rem(dp // 2, SIDE)
    u = jnp.where(core == 0, x, y)
    v = jnp.where(core == 0, y, x)
    queries, depth = query_states.shape
    blocks = negatives.shape[1]
    per_block = queries // blocks
    width = passage_last_states.shape[0]
    share = head_weight.shape[1]
    half = share // 2

    mine0 = lax.dynamic_slice_in_dim(head_weight, core * half, half, 1)
    theirs0 = lax.dynamic_slice_in_dim(head_weight, (1 - core) * half, half, 1)
    mine3 = third(mine0, 1)
    mine1 = third(mine0, -1)
    mine2 = jnp.concatenate(
        [third(mine3[: depth // 2], 1), third(mine1[depth // 2 :], -1)], axis=0
    )

    picked = lax.dynamic_index_in_dim(negatives, column, 0, keepdims=False)
    route, route0 = routes(picked, per_block, ranks)
    number = lax.broadcasted_iota(jnp.int32, (queries, 1), 0) // per_block
    facts = jnp.concatenate(
        [jnp.ones_like(number), number, positives[:, None] // 16, positives[:, None] % 16], axis=1
    ).astype(BF16)
    lead = jnp.where(column == 0, 1.0, 0.0).astype(BF16)
    facts = jnp.concatenate(
        [
            jnp.dot(route, facts, preferred_element_type=F32),
            jnp.sum(route0.astype(F32), axis=1, keepdims=True) * lead.astype(F32),
        ],
        axis=1,
    ).astype(BF16)
    facts = jnp.pad(facts, ((0, 0), (0, 128 - facts.shape[1])))
    outgoing = jnp.dot(route, query_states, preferred_element_type=F32).astype(BF16)
    outgoing = jnp.concatenate([outgoing, facts], axis=1)
    rows = outgoing.shape[0]
    received = lax.all_to_all(
        outgoing.reshape(ranks, rows // ranks, depth + 128),
        "dp",
        split_axis=0,
        concat_axis=0,
        tiled=True,
    ).reshape(rows, depth + 128)
    asked = received[:, :depth]
    facts = received[:, depth : depth + 8].astype(jnp.int32)
    valid = facts[:, 0] == 1
    block_of = facts[:, 1]
    chosen = jnp.where(facts[:, 4] == 1, facts[:, 2] * 16 + facts[:, 3], -1)

    other_states = swap(passage_last_states)
    other_asked = swap(asked)

    pieces = [mine0, mine1, mine2, mine3, theirs0, swap(mine1), swap(mine2), swap(mine3)]
    raw_p = jnp.concatenate(project(passage_last_states, pieces), axis=1)
    raw_q = jnp.concatenate(project(asked, pieces), axis=1)
    scale_p = 1.0 / jnp.sqrt(jnp.sum(raw_p * raw_p, axis=1, keepdims=True) + 1e-06)
    scale_q = 1.0 / jnp.sqrt(jnp.sum(raw_q * raw_q, axis=1, keepdims=True) + 1e-06)
    unit_p = raw_p * scale_p
    unit_q = raw_q * scale_q
    emb_p = unit_p.astype(BF16)
    emb_q = unit_q.astype(BF16)

    scores = (
        lax.dot_general(emb_q, emb_p, (((1,), (1,)), ((), ())), preferred_element_type=F32)
        * INV_TAU
    )
    target = (lax.broadcasted_iota(jnp.int32, (rows, width), 1) == chosen[:, None]).astype(F32)
    exps = jnp.exp(scores)
    sums = jnp.where(valid, jnp.sum(exps, axis=1), 0.0)
    hits = jnp.sum(scores * target, axis=1)

    spread = (
        block_of.reshape(ranks, CAP, 1, per_block)
        == lax.broadcasted_iota(jnp.int32, (1, 1, blocks, 1), 2)
    ).astype(F32)
    both = jnp.stack([sums, hits]).reshape(2, ranks, CAP, 1, per_block)
    both = jnp.sum(both * spread[None], axis=2)
    packed = both.reshape(-1, 128)
    packed = ring_sum(packed, first)
    packed = ring_sum(packed, second)
    packed = packed + swap(packed)
    packed = ring_sum(packed, third)
    both = packed.reshape(2, ranks, blocks, per_block)
    losses = (jnp.log(both[0]) - both[1]).reshape(-1)
    out_share = queries // groups
    loss_out = lax.dynamic_slice_in_dim(losses, (dp * groups + column) * out_share, out_share, 0)
    denom = jnp.sum(both[0][:, None] * spread, axis=2).reshape(rows)
    denom = jnp.where(valid, denom, 1.0)
    grads = (exps * (1.0 / denom)[:, None] - target).astype(BF16)

    d_q = jnp.dot(grads, emb_p, preferred_element_type=F32) * INV_TAU
    d_p = (
        lax.dot_general(grads, emb_q, (((0,), (0,)), ((), ())), preferred_element_type=F32)
        * INV_TAU
    )
    inner_q = jnp.sum(unit_q * d_q, axis=1, keepdims=True)
    inner_p = jnp.sum(unit_p * d_p, axis=1, keepdims=True)
    d_raw_q = ((d_q - unit_q * inner_q) * scale_q).astype(BF16)
    d_raw_p = ((d_p - unit_p * inner_p) * scale_p).astype(BF16)

    keep = SIDE * half
    d_mine = jnp.concatenate([d_raw_p[:, :keep], d_raw_q[:, :keep]], axis=0)
    d_other = swap(jnp.concatenate([d_raw_p[:, keep:], d_raw_q[:, keep:]], axis=0))
    d_all = jnp.concatenate([d_mine, d_other], axis=0)
    states = jnp.concatenate([passage_last_states, asked, other_states, other_asked], axis=0)
    part = depth // SIDE

    def term(step):
        place = lax.rem(u + step, SIDE)
        left = lax.dynamic_slice_in_dim(states, place * part, part, 1)
        return lax.dot_general(
            left, d_all, (((0,), (0,)), ((), ())), preferred_element_type=F32
        ).astype(BF16)

    summed = ring_scatter(term, first).astype(BF16)
    part2 = part // SIDE
    summed = ring_scatter(
        lambda step: lax.dynamic_slice_in_dim(summed, lax.rem(v + step, SIDE) * part2, part2, 0),
        second,
    ).astype(BF16)
    piece = ring_scatter(lambda step: summed[:, step * half : (step + 1) * half], third).astype(
        BF16
    )
    piece = ring_gather(piece, second, v)
    piece = ring_gather(piece, first, u)
    other = swap(piece)
    grad_weight = jnp.where(
        core == 0,
        jnp.concatenate([piece, other], axis=1),
        jnp.concatenate([other, piece], axis=1),
    )
    return (loss_out, grad_weight)


def solution(mesh):
    return jax.shard_map(
        shards,
        mesh=mesh,
        in_specs=(
            P("dp", None),
            P(("dp", "psg"), None),
            P(None, "psg"),
            P(None, "dp", None),
            P("dp"),
        ),
        out_specs=(P(("dp", "psg")), P(None, "psg")),
        check_vma=False,
    )
```

```python
import functools

import jax
import jax.numpy as jnp
from jax import lax
from jax.experimental import pallas as pl
from jax.experimental.pallas import tpu as pltpu
from jax.sharding import PartitionSpec as P

CAP = 2
INV_TAU = 50.0
F32 = jnp.float32
BF16 = jnp.bfloat16
SIDE = 4
VMEM = 48 * 2**20


def dp_perm(move):
    pairs = []
    for x in range(SIDE):
        for y in range(SIDE):
            for core in range(2):
                tx, ty, tcore = move(x, y, core)
                target = ((tx % SIDE) * SIDE + ty % SIDE) * 2 + tcore
                pairs.append(((x * SIDE + y) * 2 + core, target))
    return pairs


def first(value, step):
    return lax.ppermute(
        value, "dp", dp_perm(lambda x, y, k: (x + step, y, k) if k == 0 else (x, y + step, k))
    )


def second(value, step):
    return lax.ppermute(
        value, "dp", dp_perm(lambda x, y, k: (x, y + step, k) if k == 0 else (x + step, y, k))
    )


def third(value, step):
    return lax.ppermute(value, "psg", [(c, (c + step) % SIDE) for c in range(SIDE)])


def swap(value):
    return lax.ppermute(value, "dp", dp_perm(lambda x, y, k: (x, y, 1 - k)))


def ring_sum(value, move):
    return value + move(value, 1) + move(value, -1) + move(value, 2)


def dot(left, right, contract):
    return lax.dot_general(
        left, right, ((contract[:1], contract[1:]), ((), ())), preferred_element_type=F32
    )


def cost(flops, nbytes, exps=0):
    return pl.CostEstimate(flops=flops, bytes_accessed=nbytes, transcendentals=exps)


def project_kernel(pt, pb, qt, qb, mt, mb, tt, tb, out):
    first_step = pl.program_id(0) == 0
    rows = pt.shape[0]
    half = mt.shape[1]
    for row, (top, bottom) in enumerate(((pt, pb), (qt, qb))):
        for col, (wt, wb) in enumerate(((mt, mb), (tt, tb))):
            value = dot(top[...], wt[...], (1, 0)) + dot(bottom[...], wb[...], (1, 0))
            where = (pl.ds(row * rows, rows), pl.ds(col * half, half))

            @pl.when(first_step)
            def _():
                out[where] = value

            @pl.when(jnp.logical_not(first_step))
            def _():
                out[where] += value


def project(states, asked, mine, theirs):
    rows, depth = states.shape
    half = mine[0].shape[1]
    steps = SIDE
    tile = depth // 2 // steps
    top = pl.BlockSpec((rows, tile), lambda i: (0, i))
    bottom = pl.BlockSpec((rows, tile), lambda i: (0, i + steps))
    weight = pl.BlockSpec((tile, half), lambda i: (i, 0))
    return pl.pallas_call(
        project_kernel,
        grid=(steps,),
        in_specs=[top, bottom, top, bottom] + [weight] * 4,
        out_specs=pl.BlockSpec((2 * rows, 2 * half), lambda i: (0, 0)),
        out_shape=jax.ShapeDtypeStruct((2 * rows, 2 * half), F32),
        compiler_params=pltpu.CompilerParams(vmem_limit_bytes=VMEM),
        cost_estimate=cost(8 * rows * depth * half, 4 * rows * depth + 4 * depth * half + 16 * rows * half),
        name="project",
    )(states, states, asked, asked, mine[0], mine[1], theirs[0], theirs[1])


def score_kernel(r0, r1, r2, r3, chosen, valid, emb, exps, scale_out, sums, hits):
    step = pl.program_id(0)
    tile = r0.shape[0]
    width = r0.shape[1]
    rows = exps.shape[0]
    values = [r[...] for r in (r0, r1, r2, r3)]
    square = values[0] * values[0]
    for value in values[1:]:
        square = square + value * value
    scale = 1.0 / jnp.sqrt(jnp.sum(square, axis=1, keepdims=True) + 1e-06)
    scale_out[...] = scale
    for i, value in enumerate(values):
        emb[pl.ds(step * tile, tile), i * width : (i + 1) * width] = (value * scale).astype(BF16)

    @pl.when(step == pl.num_programs(0) - 1)
    def _():
        chunk = rows // SIDE
        queries = emb[rows:, :]
        total = jnp.zeros((1, queries.shape[0]), F32)
        found = jnp.zeros((1, queries.shape[0]), F32)
        for i in range(SIDE):
            part = dot(emb[i * chunk : (i + 1) * chunk, :], queries, (1, 1)) * INV_TAU
            place = lax.broadcasted_iota(jnp.int32, part.shape, 0) + i * chunk
            value = jnp.exp(part)
            exps[i * chunk : (i + 1) * chunk, :] = value
            total = total + jnp.sum(value, axis=0, keepdims=True)
            found = found + jnp.sum(
                jnp.where(place == chosen[...], part, 0.0), axis=0, keepdims=True
            )
        sums[...] = jnp.where(valid[...] == 1, total, 0.0)
        hits[...] = found


def score(raws, chosen, valid):
    both, width = raws[0].shape
    rows = both // 2
    steps = 8
    tile = both // steps
    features = width * SIDE
    raw = pl.BlockSpec((tile, width), lambda i: (i, 0))
    line = pl.BlockSpec((1, rows), lambda i: (0, 0))
    return pl.pallas_call(
        score_kernel,
        grid=(steps,),
        in_specs=[raw] * SIDE + [line] * 2,
        out_specs=[
            pl.BlockSpec((both, features), lambda i: (0, 0)),
            pl.BlockSpec((rows, rows), lambda i: (0, 0)),
            pl.BlockSpec((tile, 1), lambda i: (i, 0)),
            line,
            line,
        ],
        out_shape=[
            jax.ShapeDtypeStruct((both, features), BF16),
            jax.ShapeDtypeStruct((rows, rows), F32),
            jax.ShapeDtypeStruct((both, 1), F32),
            jax.ShapeDtypeStruct((1, rows), F32),
            jax.ShapeDtypeStruct((1, rows), F32),
        ],
        compiler_params=pltpu.CompilerParams(vmem_limit_bytes=VMEM),
        cost_estimate=cost(2 * rows * rows * features, 6 * both * features + 4 * rows * rows, rows * rows),
        name="score",
    )(*raws, chosen, valid)


def backward_kernel(emb, exps, scale, denom, chosen, mine, theirs, grads, d_emb):
    rows = exps.shape[0]
    features = emb.shape[1]
    width = features // SIDE
    half = width // 2
    inverse = 1.0 / denom[...]
    chunk = rows // SIDE
    for i in range(SIDE):
        where = slice(i * chunk, (i + 1) * chunk)
        place = lax.broadcasted_iota(jnp.int32, (chunk, rows), 0) + i * chunk
        target = jnp.where(place == chosen[...], 1.0, 0.0)
        grads[where, :] = (exps[where, :] * inverse - target).astype(BF16)
    for i in range(SIDE):
        cols = slice(i * width, (i + 1) * width)
        d_emb[:rows, cols] = dot(grads[...], emb[rows:, cols], (1, 0)) * INV_TAU
        d_emb[rows:, cols] = dot(grads[...], emb[:rows, cols], (0, 0)) * INV_TAU
    tile = 64

    @pl.loop(0, 2 * rows // tile)
    def _(step):
        where = pl.ds(pl.multiple_of(step * tile, tile), tile)
        inner = jnp.zeros((tile, 1), F32)
        for i in range(SIDE):
            cols = slice(i * width, (i + 1) * width)
            inner = inner + jnp.sum(
                emb[where, cols].astype(F32) * d_emb[where, cols], axis=1, keepdims=True
            )
        factor = scale[where, :]
        for i in range(SIDE):
            for j, out in enumerate((mine, theirs)):
                cols = slice(i * width + j * half, i * width + (j + 1) * half)
                out[where, i * half : (i + 1) * half] = (
                    (d_emb[where, cols] - emb[where, cols].astype(F32) * inner) * factor
                ).astype(BF16)


def backward(emb, exps, scale, denom, chosen):
    both, features = emb.shape
    rows = both // 2
    return pl.pallas_call(
        backward_kernel,
        out_shape=[jax.ShapeDtypeStruct((both, features // 2), BF16)] * 2,
        scratch_shapes=[pltpu.VMEM((rows, rows), BF16), pltpu.VMEM((both, features), F32)],
        compiler_params=pltpu.CompilerParams(vmem_limit_bytes=VMEM),
        cost_estimate=cost(4 * rows * rows * features, 4 * both * features + 4 * rows * rows),
        name="backward",
    )(emb, exps, scale, denom, chosen)


def weight_kernel(cols, p, q, op, oq, d, od, *outs):
    del cols
    step = pl.program_id(0)
    rows = p.shape[0]
    value = dot(p[...], d[:rows, :], (0, 0)) + dot(q[...], d[rows:, :], (0, 0))
    value = value + dot(op[...], od[:rows, :], (0, 0)) + dot(oq[...], od[rows:, :], (0, 0))
    value = value.astype(BF16)
    for i, out in enumerate(outs):

        @pl.when(step // 2 == i)
        def _():
            out[...] = value


def weight_terms(states, d_mine, d_other, u, items, part):
    rows = states[0].shape[0]
    tile = part // SIDE
    keep = d_mine.shape[1]
    cols = jnp.stack(
        [
            lax.rem(u + step, SIDE) * SIDE + part_half * 2 + t
            for step, part_half in items
            for t in range(2)
        ]
    ).astype(jnp.int32)
    state = pl.BlockSpec((rows, tile), lambda i, cols: (0, cols[i]))
    grad = pl.BlockSpec(d_mine.shape, lambda i, cols: (0, 0))
    outs = [
        pl.BlockSpec((tile, keep), lambda i, cols, j=j: (jnp.clip(i - 2 * j, 0, 1), 0))
        for j in range(len(items))
    ]
    grid_spec = pltpu.PrefetchScalarGridSpec(
        num_scalar_prefetch=1,
        grid=(2 * len(items),),
        in_specs=[state] * 4 + [grad] * 2,
        out_specs=outs,
    )
    return pl.pallas_call(
        weight_kernel,
        grid_spec=grid_spec,
        out_shape=[jax.ShapeDtypeStruct((2 * tile, keep), BF16)] * len(items),
        compiler_params=pltpu.CompilerParams(vmem_limit_bytes=VMEM),
        cost_estimate=cost(
            16 * rows * tile * keep * len(items),
            (16 * rows * tile + 4 * tile * keep) * len(items) + 8 * rows * keep,
        ),
        name="weight_terms",
    )(cols, *states, d_mine, d_other)


def place_kernel(places, *refs):
    *pieces, out, sems = refs
    count = len(pieces) // 2
    copies = []
    half = pieces[0].shape[1]
    core = places[2]
    for side in range(2):
        a = places[side]
        b = places[1 - side]
        col = pl.multiple_of(jnp.where(core == side, 0, half), half)
        for number in range(count):
            ref = pieces[side * count + number]
            rows = out.shape[0] // (SIDE * SIDE)
            for inner in range(ref.shape[0] // rows):
                far = (0, 1, 2, 2, 3)[number]
                rel = inner + (2 if number == 3 else 0)
                row = lax.rem(a + far, SIDE) * SIDE + lax.rem(b + rel, SIDE)
                copies.append(
                    pltpu.make_async_copy(
                        ref.at[pl.ds(inner * rows, rows), :],
                        out.at[pl.ds(pl.multiple_of(row * rows, rows), rows), pl.ds(col, half)],
                        sems.at[len(copies)],
                    )
                )
    for copy in copies:
        copy.start()
    for copy in copies:
        copy.wait()


def place_all(mine, other, u, v, core):
    total = SIDE * SIDE * (mine[0].shape[0] // SIDE)
    half = mine[0].shape[1]
    places = jnp.stack([u, v, core]).astype(jnp.int32)
    count = 2 * SIDE * SIDE
    return pl.pallas_call(
        place_kernel,
        in_specs=[pl.BlockSpec(memory_space=pltpu.SMEM)] + [pl.BlockSpec(memory_space=pl.ANY)] * 10,
        out_specs=pl.BlockSpec(memory_space=pl.ANY),
        out_shape=jax.ShapeDtypeStruct((total, 2 * half), BF16),
        scratch_shapes=[pltpu.SemaphoreType.DMA((count,))],
        name="place_all",
    )(places, *mine, *other)


def add(*values):
    total = values[0].astype(F32)
    for value in values[1:]:
        total = total + value.astype(F32)
    return total.astype(BF16)


def routes(mine, per_block, ranks):
    blocks, slots = mine.shape
    same = (mine[:, :, None, None] == mine[None, None, :, :]).astype(jnp.int32)
    before = (
        lax.broadcasted_iota(jnp.int32, (blocks, blocks), 1)
        < lax.broadcasted_iota(jnp.int32, (blocks, blocks), 0)
    ).astype(jnp.int32)
    place = jnp.sum(same * before[:, None, :, None], axis=(2, 3))
    line = mine * CAP + place
    rows = ranks * CAP * per_block
    line = jnp.repeat(line, per_block, axis=0)
    count = blocks * per_block
    row = lax.broadcasted_iota(jnp.int32, (rows, count), 0)
    col = lax.broadcasted_iota(jnp.int32, (rows, count), 1)
    aligned = lax.rem(row, per_block) == lax.rem(col, per_block)
    row_line = row // per_block
    hot = [aligned & (row_line == line[None, :, s]) for s in range(slots)]
    return (hot[0] | hot[1]).astype(BF16), hot[0].astype(BF16)


def shards(query_states, passage_last_states, head_weight, negatives, positives):
    ranks = lax.axis_size("dp")
    groups = lax.axis_size("psg")
    dp = lax.axis_index("dp")
    column = lax.axis_index("psg")
    core = lax.rem(dp, 2)
    x = dp // (2 * SIDE)
    y = lax.rem(dp // 2, SIDE)
    u = jnp.where(core == 0, x, y)
    v = jnp.where(core == 0, y, x)
    queries, depth = query_states.shape
    blocks = negatives.shape[1]
    per_block = queries // blocks
    share = head_weight.shape[1]
    half = share // 2
    deep = depth // 2

    def own(which, row):
        return lax.dynamic_slice(head_weight, (row * deep, which * half), (deep, half))

    mine0 = [own(core, 0), own(core, 1)]
    theirs0 = [own(1 - core, 0), own(1 - core, 1)]
    left_top = third(mine0[0], 1)
    right_bottom = third(mine0[1], -1)
    left_bottom = third(mine0[1], 1)
    right_top = third(mine0[0], -1)
    mine1 = [right_top, right_bottom]
    mine3 = [left_top, left_bottom]
    mine2 = [third(left_top, 1), third(right_bottom, -1)]

    picked = lax.dynamic_index_in_dim(negatives, column, 0, keepdims=False)
    route, route0 = routes(picked, per_block, ranks)
    number = lax.broadcasted_iota(jnp.int32, (queries, 1), 0) // per_block
    facts = jnp.concatenate(
        [jnp.ones_like(number), number, positives[:, None] // 16, positives[:, None] % 16], axis=1
    ).astype(BF16)
    lead = jnp.where(column == 0, 1.0, 0.0)
    facts = jnp.concatenate(
        [
            jnp.dot(route, facts, preferred_element_type=F32),
            jnp.sum(route0.astype(F32), axis=1, keepdims=True) * lead,
        ],
        axis=1,
    ).astype(BF16)
    facts = jnp.pad(facts, ((0, 0), (0, 128 - facts.shape[1])))
    outgoing = jnp.dot(route, query_states, preferred_element_type=F32).astype(BF16)
    outgoing = jnp.concatenate([outgoing, facts], axis=1)
    rows = outgoing.shape[0]
    asked = lax.all_to_all(
        outgoing.reshape(ranks, rows // ranks, depth + 128),
        "dp",
        split_axis=0,
        concat_axis=0,
        tiled=True,
    ).reshape(rows, depth + 128)
    facts = asked[:, depth : depth + 8].astype(jnp.int32).T
    valid = facts[0:1]
    block_of = facts[1]
    chosen = jnp.where(facts[4:5] == 1, facts[2:3] * 16 + facts[3:4], -1)

    other_states = swap(passage_last_states)
    other_asked = swap(asked)

    pieces = [
        (mine0, theirs0),
        (mine1, [swap(piece) for piece in mine1]),
        (mine2, [swap(piece) for piece in mine2]),
        (mine3, [swap(piece) for piece in mine3]),
    ]
    raws = [project(passage_last_states, asked, mine, theirs) for mine, theirs in pieces]
    emb, exps, scale, sums, hits = score(raws, chosen, valid)

    spread = (
        block_of.reshape(ranks, CAP, 1, per_block)
        == lax.broadcasted_iota(jnp.int32, (1, 1, blocks, 1), 2)
    ).astype(F32)
    both = jnp.concatenate([sums, hits], axis=0).reshape(2, ranks, CAP, 1, per_block)
    both = jnp.sum(both * spread[None], axis=2)
    packed = both.reshape(-1, blocks * per_block)
    packed = ring_sum(packed, first)
    packed = ring_sum(packed, second)
    packed = packed + swap(packed)
    packed = ring_sum(packed, third)
    both = packed.reshape(2, ranks, blocks, per_block)
    losses = (jnp.log(both[0]) - both[1]).reshape(-1)
    out_share = queries // groups
    loss_out = lax.dynamic_slice_in_dim(losses, (dp * groups + column) * out_share, out_share, 0)
    denom = jnp.sum(both[0][:, None] * spread, axis=2).reshape(1, rows)
    denom = jnp.where(valid == 1, denom, 1.0)
    d_mine, d_theirs = backward(emb, exps, scale, denom, chosen)

    d_other = swap(d_theirs)
    states = (passage_last_states, asked, other_states, other_asked)
    part = depth // SIDE
    terms = functools.partial(weight_terms, states, d_mine, d_other, u, part=part)
    far0, far1 = terms(items=[(2, 0), (2, 1)])
    from_left = first(far0, 1)
    from_right = first(far1, -1)
    right1, left0 = terms(items=[(1, 1), (3, 0)])
    left1_in = first(right1, 1)
    right0_in = first(left0, -1)
    right0, left1, own0, own1 = terms(items=[(1, 0), (3, 1), (0, 0), (0, 1)])
    left0_in = first(add(right0, from_left), 1)
    right1_in = first(add(left1, from_right), -1)
    summed = jnp.concatenate(
        [add(own0, left0_in, right0_in), add(own1, left1_in, right1_in)], axis=0
    )

    part2 = part // SIDE

    def chunk(step):
        return lax.dynamic_slice_in_dim(summed, lax.rem(v + step, SIDE) * part2, part2, 0)

    summed = add(
        chunk(0), second(chunk(1), 1), second(chunk(3), -1), second(chunk(2), 2)
    )
    cols = [summed[:, step * half : (step + 1) * half] for step in range(SIDE)]
    piece = add(cols[0], third(cols[1], 1), third(cols[3], -1), third(cols[2], 2))

    piece = jnp.concatenate(
        [piece, second(piece, -1), second(piece, 2), second(piece, 1)], axis=0
    )
    middle = piece.shape[0] // 2
    left = first(piece, 1)
    right = first(piece, -1)
    mine = [piece, right, first(left[:middle], 1), first(right[middle:], -1), left]
    other = [swap(block) for block in mine]
    return (loss_out, place_all(mine, other, u, v, core))


def solution(mesh):
    return jax.shard_map(
        shards,
        mesh=mesh,
        in_specs=(
            P("dp", None),
            P(("dp", "psg"), None),
            P(None, "psg"),
            P(None, "dp", None),
            P("dp"),
        ),
        out_specs=(P(("dp", "psg")), P(None, "psg")),
        check_vma=False,
    )
```

```python
import functools

import jax
import jax.numpy as jnp
from jax import lax
from jax.experimental import pallas as pl
from jax.experimental.pallas import tpu as pltpu
from jax.sharding import PartitionSpec as P

CAP = 2
INV_TAU = 50.0
F32 = jnp.float32
BF16 = jnp.bfloat16
SIDE = 4


def dp_perm(move):
    pairs = []
    for x in range(SIDE):
        for y in range(SIDE):
            for core in range(2):
                tx, ty, tcore = move(x, y, core)
                target = ((tx % SIDE) * SIDE + ty % SIDE) * 2 + tcore
                pairs.append(((x * SIDE + y) * 2 + core, target))
    return pairs


def first(value, step):
    return lax.ppermute(
        value, "dp", dp_perm(lambda x, y, k: (x + step, y, k) if k == 0 else (x, y + step, k))
    )


def second(value, step):
    return lax.ppermute(
        value, "dp", dp_perm(lambda x, y, k: (x, y + step, k) if k == 0 else (x + step, y, k))
    )


def third(value, step):
    return lax.ppermute(value, "psg", [(c, (c + step) % SIDE) for c in range(SIDE)])


def swap(value):
    return lax.ppermute(value, "dp", dp_perm(lambda x, y, k: (x, y, 1 - k)))


def ring_sum(value, move):
    return value + move(value, 1) + move(value, -1) + move(value, 2)


def dot(left, right, contract):
    return lax.dot_general(
        left, right, ((contract[:1], contract[1:]), ((), ())), preferred_element_type=F32
    )


def limit(mebibytes):
    return pltpu.CompilerParams(vmem_limit_bytes=mebibytes * 2**20)


def cost(flops, nbytes, exps=0):
    return pl.CostEstimate(flops=flops, bytes_accessed=nbytes, transcendentals=exps)


def project_kernel(sets, *refs):
    outs = refs[-sets[0] * sets[1] :]
    states = refs[: sets[0]]
    weights = refs[sets[0] : len(refs) - len(outs)]
    deep, half = weights[0].shape
    for i, state in enumerate(states):
        for j in range(sets[1]):
            out = outs[i * sets[1] + j]
            for col in range(2):
                top, bottom = weights[4 * j + 2 * col : 4 * j + 2 * col + 2]
                out[:, col * half : (col + 1) * half] = dot(
                    state[:, :deep], top[...], (1, 0)
                ) + dot(state[:, deep : 2 * deep], bottom[...], (1, 0))


def project(states, quarters, memory):
    rows = states[0].shape[0]
    weights = []
    specs = []
    for piece in [piece for quarter in quarters for piece in quarter]:
        deep, half = piece[-1].shape
        deep = deep * len(piece) // 2
        for i in range(2):
            place = i if len(piece) == 1 else 0
            weights.append(piece[min(i, len(piece) - 1)])
            specs.append(
                pl.BlockSpec(
                    (deep, half), lambda _, place=place: (place, 0), pipeline_mode=pl.Buffered(1)
                )
            )
    steps = 2
    state = pl.BlockSpec((rows // steps, 2 * deep), lambda i: (i, 0))
    out = pl.BlockSpec((rows // steps, 2 * half), lambda i: (i, 0))
    count = len(states) * len(quarters)
    return pl.pallas_call(
        functools.partial(project_kernel, (len(states), len(quarters))),
        grid=(steps,),
        in_specs=[state] * len(states) + specs,
        out_specs=[out] * count,
        out_shape=[jax.ShapeDtypeStruct((rows, 2 * half), F32)] * count,
        compiler_params=limit(memory),
        cost_estimate=cost(
            8 * rows * deep * half * count,
            4 * rows * deep * len(states) + 8 * deep * half * len(quarters),
        ),
        name="project",
    )(*states, *weights)


def score_kernel(*refs):
    raw_p, raw_q = refs[:SIDE], refs[SIDE : 2 * SIDE]
    chosen, valid, emb_out, exps, scale_out, sums, hits, emb = refs[2 * SIDE :]
    step = pl.program_id(0)
    tile, width = raw_p[0].shape
    rows = exps.shape[0]

    def normalise(raws):
        values = [raw[...] for raw in raws]
        square = values[0] * values[0]
        for value in values[1:]:
            square = square + value * value
        scale = 1.0 / jnp.sqrt(jnp.sum(square, axis=1, keepdims=True) + 1e-06)
        scale_out[...] = scale
        for i, value in enumerate(values):
            rounded = (value * scale).astype(BF16)
            emb[pl.ds(pl.multiple_of(step * tile, tile), tile), i * width : (i + 1) * width] = rounded
            emb_out[:, i * width : (i + 1) * width] = rounded

    @pl.when(step < rows // tile)
    def _():
        normalise(raw_p)

    @pl.when(step >= rows // tile)
    def _():
        normalise(raw_q)

    @pl.when(step == pl.num_programs(0) - 1)
    def _():
        chunk = rows // SIDE
        queries = emb[rows:, :]
        total = jnp.zeros((1, queries.shape[0]), F32)
        found = jnp.zeros((1, queries.shape[0]), F32)
        for i in range(SIDE):
            part = dot(emb[i * chunk : (i + 1) * chunk, :], queries, (1, 1)) * INV_TAU
            place = lax.broadcasted_iota(jnp.int32, part.shape, 0) + i * chunk
            value = jnp.exp(part)
            exps[i * chunk : (i + 1) * chunk, :] = value
            total = total + jnp.sum(value, axis=0, keepdims=True)
            found = found + jnp.sum(
                jnp.where(place == chosen[...], part, 0.0), axis=0, keepdims=True
            )
        sums[...] = jnp.where(valid[...] == 1, total, 0.0)
        hits[...] = found


def score(raws, raws_q, chosen, valid):
    rows, width = raws[0].shape
    both = 2 * rows
    steps = 8
    tile = both // steps
    features = width * SIDE
    raw_p = pl.BlockSpec((tile, width), lambda i: (jnp.minimum(i, rows // tile - 1), 0))
    raw_q = pl.BlockSpec((tile, width), lambda i: (jnp.maximum(i - rows // tile, 0), 0))
    line = pl.BlockSpec((1, rows), lambda i: (0, 0))
    return pl.pallas_call(
        score_kernel,
        grid=(steps,),
        in_specs=[raw_p] * SIDE + [raw_q] * SIDE + [line] * 2,
        out_specs=[
            pl.BlockSpec((tile, features), lambda i: (i, 0)),
            pl.BlockSpec((rows, rows), lambda i: (0, 0)),
            pl.BlockSpec((tile, 1), lambda i: (i, 0)),
            line,
            line,
        ],
        out_shape=[
            jax.ShapeDtypeStruct((both, features), BF16),
            jax.ShapeDtypeStruct((rows, rows), F32),
            jax.ShapeDtypeStruct((both, 1), F32),
            jax.ShapeDtypeStruct((1, rows), F32),
            jax.ShapeDtypeStruct((1, rows), F32),
        ],
        scratch_shapes=[pltpu.VMEM((both, features), BF16)],
        compiler_params=limit(20),
        cost_estimate=cost(2 * rows * rows * features, 6 * both * features + 4 * rows * rows, rows * rows),
        name="score",
    )(*raws, *raws_q, chosen, valid)


def backward_kernel(emb, exps, scale, denom, chosen, mine, theirs, grads, d_emb):
    rows = exps.shape[0]
    features = emb.shape[1]
    width = features // SIDE
    half = width // 2
    inverse = 1.0 / denom[...]
    chunk = rows // SIDE
    for i in range(SIDE):
        where = slice(i * chunk, (i + 1) * chunk)
        place = lax.broadcasted_iota(jnp.int32, (chunk, rows), 0) + i * chunk
        target = jnp.where(place == chosen[...], 1.0, 0.0)
        grads[where, :] = (exps[where, :] * inverse - target).astype(BF16)
    for i in range(SIDE):
        cols = slice(i * width, (i + 1) * width)
        d_emb[:rows, cols] = dot(grads[...], emb[rows:, cols], (1, 0)) * INV_TAU
        d_emb[rows:, cols] = dot(grads[...], emb[:rows, cols], (0, 0)) * INV_TAU
    tile = 64

    @pl.loop(0, 2 * rows // tile)
    def _(step):
        where = pl.ds(pl.multiple_of(step * tile, tile), tile)
        inner = jnp.zeros((tile, 1), F32)
        for i in range(SIDE):
            cols = slice(i * width, (i + 1) * width)
            inner = inner + jnp.sum(
                emb[where, cols].astype(F32) * d_emb[where, cols], axis=1, keepdims=True
            )
        factor = scale[where, :]
        for i in range(SIDE):
            for j, out in enumerate((mine, theirs)):
                cols = slice(i * width + j * half, i * width + (j + 1) * half)
                out[where, i * half : (i + 1) * half] = (
                    (d_emb[where, cols] - emb[where, cols].astype(F32) * inner) * factor
                ).astype(BF16)


def backward(emb, exps, scale, denom, chosen):
    both, features = emb.shape
    rows = both // 2
    return pl.pallas_call(
        backward_kernel,
        out_shape=[jax.ShapeDtypeStruct((both, features // 2), BF16)] * 2,
        scratch_shapes=[pltpu.VMEM((rows, rows), BF16), pltpu.VMEM((both, features), F32)],
        compiler_params=limit(20),
        cost_estimate=cost(4 * rows * rows * features, 4 * both * features + 4 * rows * rows),
        name="backward",
    )(emb, exps, scale, denom, chosen)


def weight_kernel(cols, p, q, op, oq, d, od, *outs):
    del cols
    step = pl.program_id(0)
    rows = p.shape[0]
    value = dot(p[...], d[:rows, :], (0, 0)) + dot(q[...], d[rows:, :], (0, 0))
    value = value + dot(op[...], od[:rows, :], (0, 0)) + dot(oq[...], od[rows:, :], (0, 0))
    value = value.astype(BF16)
    for i, out in enumerate(outs):

        @pl.when(step // 2 == i)
        def _():
            out[...] = value


def weight_terms(states, d_mine, d_other, u, items, part):
    rows = states[0].shape[0]
    tile = part // SIDE
    keep = d_mine.shape[1]
    cols = jnp.stack(
        [
            lax.rem(u + step, SIDE) * SIDE + part_half * 2 + t
            for step, part_half in items
            for t in range(2)
        ]
    ).astype(jnp.int32)
    state = pl.BlockSpec((rows, tile), lambda i, cols: (0, cols[i]))
    grad = pl.BlockSpec(d_mine.shape, lambda i, cols: (0, 0))
    outs = [
        pl.BlockSpec((tile, keep), lambda i, cols, j=j: (jnp.clip(i - 2 * j, 0, 1), 0))
        for j in range(len(items))
    ]
    grid_spec = pltpu.PrefetchScalarGridSpec(
        num_scalar_prefetch=1,
        grid=(2 * len(items),),
        in_specs=[state] * 4 + [grad] * 2,
        out_specs=outs,
    )
    return pl.pallas_call(
        weight_kernel,
        grid_spec=grid_spec,
        out_shape=[jax.ShapeDtypeStruct((2 * tile, keep), BF16)] * len(items),
        compiler_params=limit(17),
        cost_estimate=cost(
            16 * rows * tile * keep * len(items),
            (16 * rows * tile + 4 * tile * keep) * len(items) + 8 * rows * keep,
        ),
        name="weight_terms",
    )(cols, *states, d_mine, d_other)


def place_kernel(places, *refs):
    *pieces, out = refs
    count = len(pieces) // 2
    half = pieces[0].shape[1]
    rows = out.shape[0] // (SIDE * SIDE)
    core = places[2]
    for side in range(2):
        a = places[side]
        b = places[1 - side]

        def fill(column, side=side, a=a, b=b):
            for number in range(count):
                ref = pieces[side * count + number]
                for inner in range(ref.shape[0] // rows):
                    far = (0, 1, 2, 2, 3)[number]
                    rel = inner + (2 if number == 3 else 0)
                    row = lax.rem(a + far, SIDE) * SIDE + lax.rem(b + rel, SIDE)
                    out[pl.ds(pl.multiple_of(row * rows, rows), rows), column * half : (column + 1) * half] = (
                        ref[inner * rows : (inner + 1) * rows, :]
                    )

        @pl.when(core == 0)
        def _():
            fill(side)

        @pl.when(core != 0)
        def _():
            fill(1 - side)


def place_all(mine, other, u, v, core):
    total = SIDE * SIDE * (mine[0].shape[0] // SIDE)
    half = mine[0].shape[1]
    places = jnp.stack([u, v, core]).astype(jnp.int32)
    return pl.pallas_call(
        place_kernel,
        in_specs=[pl.BlockSpec(memory_space=pltpu.SMEM)] + [pl.BlockSpec(memory_space=pltpu.VMEM)] * 10,
        out_specs=pl.BlockSpec(memory_space=pltpu.VMEM),
        out_shape=jax.ShapeDtypeStruct((total, 2 * half), BF16),
        compiler_params=limit(14),
        name="place_all",
    )(places, *mine, *other)


def add(*values):
    total = values[0].astype(F32)
    for value in values[1:]:
        total = total + value.astype(F32)
    return total.astype(BF16)


def routes(mine, per_block, ranks):
    blocks, slots = mine.shape
    same = (mine[:, :, None, None] == mine[None, None, :, :]).astype(jnp.int32)
    before = (
        lax.broadcasted_iota(jnp.int32, (blocks, blocks), 1)
        < lax.broadcasted_iota(jnp.int32, (blocks, blocks), 0)
    ).astype(jnp.int32)
    place = jnp.sum(same * before[:, None, :, None], axis=(2, 3))
    line = mine * CAP + place
    rows = ranks * CAP * per_block
    line = jnp.repeat(line, per_block, axis=0)
    count = blocks * per_block
    row = lax.broadcasted_iota(jnp.int32, (rows, count), 0)
    col = lax.broadcasted_iota(jnp.int32, (rows, count), 1)
    aligned = lax.rem(row, per_block) == lax.rem(col, per_block)
    row_line = row // per_block
    hot = [aligned & (row_line == line[None, :, s]) for s in range(slots)]
    return (hot[0] | hot[1]).astype(BF16), hot[0].astype(BF16)


def shards(query_states, passage_last_states, head_weight, negatives, positives):
    ranks = lax.axis_size("dp")
    groups = lax.axis_size("psg")
    dp = lax.axis_index("dp")
    column = lax.axis_index("psg")
    core = lax.rem(dp, 2)
    x = dp // (2 * SIDE)
    y = lax.rem(dp // 2, SIDE)
    u = jnp.where(core == 0, x, y)
    v = jnp.where(core == 0, y, x)
    queries, depth = query_states.shape
    blocks = negatives.shape[1]
    per_block = queries // blocks
    share = head_weight.shape[1]
    half = share // 2
    deep = depth // 2

    def own(which):
        return lax.dynamic_slice_in_dim(head_weight, which * half, half, 1)

    mine0, query_states = lax.optimization_barrier((own(core), query_states))
    mine3 = third(mine0, 1)
    mine1 = third(mine0, -1)
    theirs0 = own(1 - core)
    (raw_p0,) = project([passage_last_states], [([mine0], [theirs0])], 14)
    mine1, mine3, raw_p0 = lax.optimization_barrier((mine1, mine3, raw_p0))
    theirs1 = swap(mine1)
    theirs3 = swap(mine3)
    mine2 = [third(mine3[:deep], 1), third(mine1[deep:], -1)]

    picked = lax.dynamic_index_in_dim(negatives, column, 0, keepdims=False)
    route, route0 = routes(picked, per_block, ranks)
    number = lax.broadcasted_iota(jnp.int32, (queries, 1), 0) // per_block
    facts = jnp.concatenate(
        [jnp.ones_like(number), number, positives[:, None] // 16, positives[:, None] % 16], axis=1
    ).astype(BF16)
    lead = jnp.where(column == 0, 1.0, 0.0)
    facts = jnp.concatenate(
        [
            jnp.dot(route, facts, preferred_element_type=F32),
            jnp.sum(route0.astype(F32), axis=1, keepdims=True) * lead,
        ],
        axis=1,
    ).astype(BF16)
    facts = jnp.pad(facts, ((0, 0), (0, 128 - facts.shape[1])))
    outgoing = jnp.dot(route, query_states, preferred_element_type=F32).astype(BF16)
    outgoing = jnp.concatenate([outgoing, facts], axis=1)
    rows = outgoing.shape[0]
    asked = lax.all_to_all(
        outgoing.reshape(ranks, rows // ranks, depth + 128),
        "dp",
        split_axis=0,
        concat_axis=0,
        tiled=True,
    ).reshape(rows, depth + 128)
    facts = asked[:, depth : depth + 8].astype(jnp.int32).T
    valid = facts[0:1]
    block_of = facts[1]
    chosen = jnp.where(facts[4:5] == 1, facts[2:3] * 16 + facts[3:4], -1)

    other_states = swap(passage_last_states)
    other_asked = swap(asked)

    near = [([mine1], [theirs1]), ([mine3], [theirs3])]
    raw_p1, raw_p3 = project([passage_last_states], near, 20)
    asked, raw_p0, raw_p1, raw_p3 = lax.optimization_barrier((asked, raw_p0, raw_p1, raw_p3))
    raw_q0, raw_q1, raw_q3 = project([asked], [([mine0], [theirs0]), *near], 26)
    *mine2, raw_q0, raw_q1, raw_q3 = lax.optimization_barrier((*mine2, raw_q0, raw_q1, raw_q3))
    theirs2 = [swap(piece) for piece in mine2]
    raw_p2, raw_q2 = project([passage_last_states, asked], [(mine2, theirs2)], 18)
    emb, exps, scale, sums, hits = score(
        (raw_p0, raw_p1, raw_p2, raw_p3), (raw_q0, raw_q1, raw_q2, raw_q3), chosen, valid
    )

    spread = (
        block_of.reshape(ranks, CAP, 1, per_block)
        == lax.broadcasted_iota(jnp.int32, (1, 1, blocks, 1), 2)
    ).astype(F32)
    both = jnp.concatenate([sums, hits], axis=0).reshape(2, ranks, CAP, 1, per_block)
    both = jnp.sum(both * spread[None], axis=2)
    packed = both.reshape(-1, blocks * per_block)
    packed = ring_sum(packed, first)
    packed = ring_sum(packed, second)
    packed = packed + swap(packed)
    packed = ring_sum(packed, third)
    both = packed.reshape(2, ranks, blocks, per_block)
    losses = (jnp.log(both[0]) - both[1]).reshape(-1)
    out_share = queries // groups
    loss_out = lax.dynamic_slice_in_dim(losses, (dp * groups + column) * out_share, out_share, 0)
    denom = jnp.sum(both[0][:, None] * spread, axis=2).reshape(1, rows)
    denom = jnp.where(valid == 1, denom, 1.0)
    d_mine, d_theirs = backward(emb, exps, scale, denom, chosen)

    d_other = swap(d_theirs)
    states = (passage_last_states, asked, other_states, other_asked)
    part = depth // SIDE
    terms = functools.partial(weight_terms, states, d_mine, d_other, u, part=part)
    (far0,) = terms(items=[(2, 0)])
    from_left = first(far0, 1)
    (far1,) = terms(items=[(2, 1)])
    from_right = first(far1, -1)
    right1, left0 = terms(items=[(1, 1), (3, 0)])
    left1_in = first(right1, 1)
    right0_in = first(left0, -1)
    right0, left1 = terms(items=[(1, 0), (3, 1)])
    left0_in = first(add(right0, from_left), 1)
    right1_in = first(add(left1, from_right), -1)
    own0, own1 = terms(items=[(0, 0), (0, 1)])
    summed = jnp.concatenate(
        [add(own0, left0_in, right0_in), add(own1, left1_in, right1_in)], axis=0
    )

    part2 = part // SIDE

    def chunk(step):
        return lax.dynamic_slice_in_dim(summed, lax.rem(v + step, SIDE) * part2, part2, 0)

    summed = add(
        chunk(0), second(chunk(1), 1), second(chunk(3), -1), second(chunk(2), 2)
    )
    cols = [summed[:, step * half : (step + 1) * half] for step in range(SIDE)]
    piece = add(cols[0], third(cols[1], 1), third(cols[3], -1), third(cols[2], 2))

    piece = jnp.concatenate(
        [piece, second(piece, -1), second(piece, 2), second(piece, 1)], axis=0
    )
    middle = piece.shape[0] // 2
    left = first(piece, 1)
    right = first(piece, -1)
    mine = [piece, right, first(left[:middle], 1), first(right[middle:], -1), left]
    other = [swap(block) for block in mine]
    return (loss_out, place_all(mine, other, u, v, core))


def solution(mesh):
    return jax.shard_map(
        shards,
        mesh=mesh,
        in_specs=(
            P("dp", None),
            P(("dp", "psg"), None),
            P(None, "psg"),
            P(None, "dp", None),
            P("dp"),
        ),
        out_specs=(P(("dp", "psg")), P(None, "psg")),
        check_vma=False,
    )
```

```python
import functools

import jax
import jax.numpy as jnp
from jax import lax
from jax.experimental import pallas as pl
from jax.experimental.pallas import tpu as pltpu
from jax.sharding import PartitionSpec as P

CAP = 2
INV_TAU = 50.0
F32 = jnp.float32
BF16 = jnp.bfloat16
SIDE = 4
COVER = 6.0


def dp_perm(move):
    pairs = []
    for x in range(SIDE):
        for y in range(SIDE):
            for core in range(2):
                tx, ty, tcore = move(x, y, core)
                target = ((tx % SIDE) * SIDE + ty % SIDE) * 2 + tcore
                pairs.append(((x * SIDE + y) * 2 + core, target))
    return pairs


def first(value, step):
    return lax.ppermute(
        value, "dp", dp_perm(lambda x, y, k: (x + step, y, k) if k == 0 else (x, y + step, k))
    )


def second(value, step):
    return lax.ppermute(
        value, "dp", dp_perm(lambda x, y, k: (x, y + step, k) if k == 0 else (x + step, y, k))
    )


def third(value, step):
    return lax.ppermute(value, "psg", [(c, (c + step) % SIDE) for c in range(SIDE)])


def swap(value):
    return lax.ppermute(value, "dp", dp_perm(lambda x, y, k: (x, y, 1 - k)))


def ring_sum(value, move):
    return value + move(value, 1) + move(value, -1) + move(value, 2)


def dot(left, right, contract):
    return lax.dot_general(
        left, right, ((contract[:1], contract[1:]), ((), ())), preferred_element_type=F32
    )


def limit(mebibytes):
    return pltpu.CompilerParams(vmem_limit_bytes=mebibytes * 2**20)


def in_hbm(value):
    return pltpu.with_memory_space_constraint(value, pltpu.HBM)


def cost(flops, nbytes, exps=0):
    return pl.CostEstimate(flops=flops, bytes_accessed=nbytes, transcendentals=exps)


def project_kernel(sets, _, *refs):
    outs = refs[-sets[0] * sets[1] :]
    states = refs[: sets[0]]
    weights = refs[sets[0] : len(refs) - len(outs)]
    deep, half = weights[0].shape
    for i, state in enumerate(states):
        for j in range(sets[1]):
            out = outs[i * sets[1] + j]
            for col in range(2):
                top, bottom = weights[4 * j + 2 * col : 4 * j + 2 * col + 2]
                out[:, col * half : (col + 1) * half] = dot(
                    state[:, :deep], top[...], (1, 0)
                ) + dot(state[:, deep : 2 * deep], bottom[...], (1, 0))


def project(states, quarters, core, memory, weight=1.0):
    rows = states[0].shape[0]
    weights = []
    specs = []
    for quarter in quarters:
        for side in range(2):
            for i in range(2):
                if isinstance(quarter, list):
                    weights.append(quarter[side][i])
                    deep, half = weights[-1].shape
                    place = lambda _, core: (0, 0)
                else:
                    weights.append(quarter)
                    deep, half = quarter.shape[0] // 2, quarter.shape[1] // 2
                    place = lambda _, core, i=i, side=side: (i, core[side])
                specs.append(pl.BlockSpec((deep, half), place, pipeline_mode=pl.Buffered(1)))
    steps = 2
    state = pl.BlockSpec((rows // steps, 2 * deep), lambda i, core: (i, 0))
    out = pl.BlockSpec((rows // steps, 2 * half), lambda i, core: (i, 0))
    count = len(states) * len(quarters)
    return pl.pallas_call(
        functools.partial(project_kernel, (len(states), len(quarters))),
        grid_spec=pltpu.PrefetchScalarGridSpec(
            num_scalar_prefetch=1,
            grid=(steps,),
            in_specs=[state] * len(states) + specs,
            out_specs=[out] * count,
        ),
        out_shape=[pltpu.HBM((rows, 2 * half), F32)] * count,
        compiler_params=limit(memory),
        cost_estimate=cost(
            int(weight * 8 * rows * deep * half * count),
            4 * rows * deep * len(states) + 8 * deep * half * len(quarters),
        ),
        name="project",
    )(core, *map(in_hbm, states), *map(in_hbm, weights))


def score_kernel(*refs):
    raw_p, raw_q = refs[:SIDE], refs[SIDE : 2 * SIDE]
    chosen, valid, emb_out, exps, scale_out, sums, hits, emb = refs[2 * SIDE :]
    step = pl.program_id(0)
    tile, width = raw_p[0].shape
    rows = exps.shape[0]

    def normalise(raws):
        values = [raw[...] for raw in raws]
        square = values[0] * values[0]
        for value in values[1:]:
            square = square + value * value
        scale = 1.0 / jnp.sqrt(jnp.sum(square, axis=1, keepdims=True) + 1e-06)
        scale_out[...] = scale
        for i, value in enumerate(values):
            rounded = (value * scale).astype(BF16)
            emb[pl.ds(pl.multiple_of(step * tile, tile), tile), i * width : (i + 1) * width] = rounded
            emb_out[:, i * width : (i + 1) * width] = rounded

    @pl.when(step < rows // tile)
    def _():
        normalise(raw_p)

    @pl.when(step >= rows // tile)
    def _():
        normalise(raw_q)

    @pl.when(step == pl.num_programs(0) - 1)
    def _():
        chunk = rows // SIDE
        queries = emb[rows:, :]
        total = jnp.zeros((1, queries.shape[0]), F32)
        found = jnp.zeros((1, queries.shape[0]), F32)
        for i in range(SIDE):
            part = dot(emb[i * chunk : (i + 1) * chunk, :], queries, (1, 1)) * INV_TAU
            place = lax.broadcasted_iota(jnp.int32, part.shape, 0) + i * chunk
            value = jnp.exp(part)
            exps[i * chunk : (i + 1) * chunk, :] = value
            total = total + jnp.sum(value, axis=0, keepdims=True)
            found = found + jnp.sum(
                jnp.where(place == chosen[...], part, 0.0), axis=0, keepdims=True
            )
        sums[...] = jnp.where(valid[...] == 1, total, 0.0)
        hits[...] = found


def score(raws, raws_q, chosen, valid):
    rows, width = raws[0].shape
    both = 2 * rows
    steps = 8
    tile = both // steps
    features = width * SIDE
    raw_p = pl.BlockSpec((tile, width), lambda i: (jnp.minimum(i, rows // tile - 1), 0))
    raw_q = pl.BlockSpec((tile, width), lambda i: (jnp.maximum(i - rows // tile, 0), 0))
    line = pl.BlockSpec((1, rows), lambda i: (0, 0))
    return pl.pallas_call(
        score_kernel,
        grid=(steps,),
        in_specs=[raw_p] * SIDE + [raw_q] * SIDE + [line] * 2,
        out_specs=[
            pl.BlockSpec((tile, features), lambda i: (i, 0)),
            pl.BlockSpec((rows, rows), lambda i: (0, 0)),
            pl.BlockSpec((tile, 1), lambda i: (i, 0)),
            line,
            line,
        ],
        out_shape=[
            pltpu.HBM((both, features), BF16),
            pltpu.HBM((rows, rows), F32),
            pltpu.HBM((both, 1), F32),
            jax.ShapeDtypeStruct((1, rows), F32),
            jax.ShapeDtypeStruct((1, rows), F32),
        ],
        scratch_shapes=[pltpu.VMEM((both, features), BF16)],
        compiler_params=limit(15),
        cost_estimate=cost(2 * rows * rows * features, 6 * both * features + 4 * rows * rows, rows * rows),
        name="score",
    )(*raws, *raws_q, chosen, valid)


def backward_kernel(emb, exps, scale, denom, chosen, mine, theirs, grads, d_emb):
    rows = exps.shape[0]
    features = emb.shape[1]
    width = features // SIDE
    half = width // 2
    inverse = 1.0 / denom[...]
    chunk = rows // SIDE
    for i in range(SIDE):
        where = slice(i * chunk, (i + 1) * chunk)
        place = lax.broadcasted_iota(jnp.int32, (chunk, rows), 0) + i * chunk
        target = jnp.where(place == chosen[...], 1.0, 0.0)
        grads[where, :] = (exps[where, :] * inverse - target).astype(BF16)
    for i in range(SIDE):
        cols = slice(i * width, (i + 1) * width)
        d_emb[:rows, cols] = dot(grads[...], emb[rows:, cols], (1, 0)) * INV_TAU
        d_emb[rows:, cols] = dot(grads[...], emb[:rows, cols], (0, 0)) * INV_TAU
    tile = 64

    @pl.loop(0, 2 * rows // tile)
    def _(step):
        where = pl.ds(pl.multiple_of(step * tile, tile), tile)
        inner = jnp.zeros((tile, 1), F32)
        for i in range(SIDE):
            cols = slice(i * width, (i + 1) * width)
            inner = inner + jnp.sum(
                emb[where, cols].astype(F32) * d_emb[where, cols], axis=1, keepdims=True
            )
        factor = scale[where, :]
        for i in range(SIDE):
            for j, out in enumerate((mine, theirs)):
                cols = slice(i * width + j * half, i * width + (j + 1) * half)
                out[where, i * half : (i + 1) * half] = (
                    (d_emb[where, cols] - emb[where, cols].astype(F32) * inner) * factor
                ).astype(BF16)


def backward(emb, exps, scale, denom, chosen):
    both, features = emb.shape
    rows = both // 2
    return pl.pallas_call(
        backward_kernel,
        out_shape=[jax.ShapeDtypeStruct((both, features // 2), BF16)] * 2,
        scratch_shapes=[pltpu.VMEM((rows, rows), BF16), pltpu.VMEM((both, features), F32)],
        compiler_params=limit(20),
        cost_estimate=cost(4 * rows * rows * features, 4 * both * features + 4 * rows * rows),
        name="backward",
    )(in_hbm(emb), in_hbm(exps), in_hbm(scale), denom, chosen)


def weight_kernel(joined, cols, p, q, op, oq, d, od, *refs):
    del cols
    step = pl.program_id(0)
    items = 2
    outs = refs[-1:] if joined else refs[-items:]
    added = refs[: len(refs) - len(outs)]
    rows = p.shape[0]
    value = dot(p[...], d[:rows, :], (0, 0)) + dot(q[...], d[rows:, :], (0, 0))
    value = value + dot(op[...], od[:rows, :], (0, 0)) + dot(oq[...], od[rows:, :], (0, 0))
    for i in range(items):

        @pl.when(step == i)
        def _():
            total = value + added[i][...].astype(F32) if added else value
            outs[0 if joined else i][...] = total.astype(BF16)


def weight_terms(states, d_mine, d_other, u, items, part, added=(), joined=False):
    rows = states[0].shape[0]
    tile = part // 2
    keep = d_mine.shape[1]
    count = len(items)
    cols = jnp.stack([lax.rem(u + step, SIDE) * 2 + half for step, half in items])
    state = pl.BlockSpec((rows, tile), lambda i, cols: (0, cols[i]))

    def once(shape):
        return pl.BlockSpec(shape, lambda i, cols: (0, 0), pipeline_mode=pl.Buffered(1))

    if joined:
        out_specs = [pl.BlockSpec((tile, keep), lambda i, cols: (i, 0))]
        out_shape = [jax.ShapeDtypeStruct((count * tile, keep), BF16)]
    else:
        out_specs = [pl.BlockSpec((tile, keep), lambda i, cols: (0, 0))] * count
        out_shape = [jax.ShapeDtypeStruct((tile, keep), BF16)] * count
    return pl.pallas_call(
        functools.partial(weight_kernel, joined),
        grid_spec=pltpu.PrefetchScalarGridSpec(
            num_scalar_prefetch=1,
            grid=(count,),
            in_specs=[state] * 4 + [once(d_mine.shape)] * 2 + [once((tile, keep))] * len(added),
            out_specs=out_specs,
        ),
        out_shape=out_shape,
        compiler_params=limit(16 + 2 * count + len(added)),
        cost_estimate=cost(
            2 * rows * tile * keep * count, (2 * rows * tile + tile * keep) * count
        ),
        name="weight_terms",
    )(cols.astype(jnp.int32), *states, d_mine, d_other, *added)


def place_kernel(places, *refs):
    *pieces, out = refs
    count = len(pieces) // 2
    half = pieces[0].shape[1]
    rows = out.shape[0] // (SIDE * SIDE)
    core = places[2]
    for side in range(2):
        a = places[side]
        b = places[1 - side]

        def fill(column, side=side, a=a, b=b):
            for number in range(count):
                ref = pieces[side * count + number]
                for inner in range(ref.shape[0] // rows):
                    far = (0, 1, 2, 2, 3)[number]
                    rel = inner + (2 if number == 3 else 0)
                    row = lax.rem(a + far, SIDE) * SIDE + lax.rem(b + rel, SIDE)
                    out[pl.ds(pl.multiple_of(row * rows, rows), rows), column * half : (column + 1) * half] = (
                        ref[inner * rows : (inner + 1) * rows, :]
                    )

        @pl.when(core == 0)
        def _():
            fill(side)

        @pl.when(core != 0)
        def _():
            fill(1 - side)


def place_all(mine, other, u, v, core):
    total = SIDE * SIDE * (mine[0].shape[0] // SIDE)
    half = mine[0].shape[1]
    places = jnp.stack([u, v, core]).astype(jnp.int32)
    return pl.pallas_call(
        place_kernel,
        in_specs=[pl.BlockSpec(memory_space=pltpu.SMEM)] + [pl.BlockSpec(memory_space=pltpu.VMEM)] * 10,
        out_specs=pl.BlockSpec(memory_space=pltpu.VMEM),
        out_shape=jax.ShapeDtypeStruct((total, 2 * half), BF16),
        compiler_params=limit(10),
        name="place_all",
    )(places, *mine, *other)


def add(*values):
    total = values[0].astype(F32)
    for value in values[1:]:
        total = total + value.astype(F32)
    return total.astype(BF16)


def lines_of(mine, per_block):
    blocks, _ = mine.shape
    same = (mine[:, :, None, None] == mine[None, None, :, :]).astype(jnp.int32)
    before = (
        lax.broadcasted_iota(jnp.int32, (blocks, blocks), 1)
        < lax.broadcasted_iota(jnp.int32, (blocks, blocks), 0)
    ).astype(jnp.int32)
    place = jnp.sum(same * before[:, None, :, None], axis=(2, 3))
    return jnp.repeat((mine * CAP + place).T, per_block, axis=1)


def route_kernel(per_block, lines, states, facts, lead_facts, out):
    tile = out.shape[0]
    queries, depth = states.shape
    row = lax.broadcasted_iota(jnp.int32, (tile, queries), 0) + pl.program_id(0) * tile
    col = lax.broadcasted_iota(jnp.int32, (tile, queries), 1)
    aligned = jnp.bitwise_and(row, per_block - 1) == jnp.bitwise_and(col, per_block - 1)
    line = jnp.right_shift(row, per_block.bit_length() - 1)
    lead = aligned & (line == lines[0:1, :])
    both = lead | (aligned & (line == lines[1:2, :]))
    lead = jnp.where(lead, 1.0, 0.0).astype(BF16)
    both = jnp.where(both, 1.0, 0.0).astype(BF16)
    out[:, :depth] = dot(both, states[...], (1, 0)).astype(BF16)
    out[:, depth:] = (
        dot(both, facts[...], (1, 0)) + dot(lead, lead_facts[...], (1, 0))
    ).astype(BF16)


def route(lines, states, facts, lead_facts, rows, per_block):
    queries, depth = states.shape
    steps = 4
    wide = depth + facts.shape[1]

    def whole(value):
        return pl.BlockSpec(value.shape, lambda i: (0, 0))

    return pl.pallas_call(
        functools.partial(route_kernel, per_block),
        grid=(steps,),
        in_specs=[whole(value) for value in (lines, states, facts, lead_facts)],
        out_specs=pl.BlockSpec((rows // steps, wide), lambda i: (i, 0)),
        out_shape=jax.ShapeDtypeStruct((rows, wide), BF16),
        compiler_params=limit(10),
        cost_estimate=cost(2 * rows * queries * wide, 2 * (rows + queries) * wide),
        name="route",
    )(lines, states, facts, lead_facts)


def shards(query_states, passage_last_states, head_weight, negatives, positives):
    ranks = lax.axis_size("dp")
    groups = lax.axis_size("psg")
    dp = lax.axis_index("dp")
    column = lax.axis_index("psg")
    core = lax.rem(dp, 2)
    x = dp // (2 * SIDE)
    y = lax.rem(dp // 2, SIDE)
    u = jnp.where(core == 0, x, y)
    v = jnp.where(core == 0, y, x)
    queries, depth = query_states.shape
    blocks = negatives.shape[1]
    per_block = queries // blocks
    share = head_weight.shape[1]
    half = share // 2
    deep = depth // 2

    def own(row):
        return lax.dynamic_slice(head_weight, (row * deep, core * half), (deep, half))

    top, bottom, query_states = lax.optimization_barrier((own(0), own(1), query_states))
    left_top = third(top, 1)
    right_bottom = third(bottom, -1)
    left_bottom = third(bottom, 1)
    right_top = third(top, -1)
    sides = jnp.stack([core, 1 - core]).astype(jnp.int32)
    (raw_p0,) = project([passage_last_states], [head_weight], sides, 12)
    left_top, left_bottom, right_top, right_bottom, raw_p0 = lax.optimization_barrier(
        (left_top, left_bottom, right_top, right_bottom, raw_p0)
    )
    mine1 = [right_top, right_bottom]
    mine3 = [left_top, left_bottom]
    theirs1 = [swap(piece) for piece in mine1]
    theirs3 = [swap(piece) for piece in mine3]
    mine2 = [third(left_top, 1), third(right_bottom, -1)]

    picked = lax.dynamic_index_in_dim(negatives, column, 0, keepdims=False)
    lines = lines_of(picked, per_block)
    number = lax.broadcasted_iota(jnp.int32, (queries, 1), 0) // per_block
    facts = jnp.concatenate(
        [jnp.ones_like(number), number, positives[:, None] // 16, positives[:, None] % 16], axis=1
    ).astype(BF16)
    facts = jnp.pad(facts, ((0, 0), (0, 128 - facts.shape[1])))
    lead_facts = (
        (lax.broadcasted_iota(jnp.int32, facts.shape, 1) == 4) & (column == 0)
    ).astype(BF16)
    rows = ranks * CAP * per_block
    outgoing = route(lines, query_states, facts, lead_facts, rows, per_block)
    asked = lax.all_to_all(
        outgoing.reshape(ranks, rows // ranks, depth + 128),
        "dp",
        split_axis=0,
        concat_axis=0,
        tiled=True,
    ).reshape(rows, depth + 128)
    facts = asked[:, depth : depth + 8].astype(jnp.int32).T
    valid = facts[0:1]
    block_of = facts[1]
    chosen = jnp.where(facts[4:5] == 1, facts[2:3] * 16 + facts[3:4], -1)

    other_states = swap(passage_last_states)
    other_asked = swap(asked)

    near = [[mine1, theirs1], [mine3, theirs3]]
    raw_p1, raw_p3 = project([passage_last_states], near, sides, 17, COVER)
    asked, raw_p0, raw_p1, raw_p3 = lax.optimization_barrier((asked, raw_p0, raw_p1, raw_p3))
    raw_q0, raw_q1, raw_q3 = project([asked], [head_weight, *near], sides, 22)
    *mine2, raw_q0, raw_q1, raw_q3 = lax.optimization_barrier((*mine2, raw_q0, raw_q1, raw_q3))
    theirs2 = [swap(piece) for piece in mine2]
    raw_p2, raw_q2 = project([passage_last_states, asked], [[mine2, theirs2]], sides, 17)
    emb, exps, scale, sums, hits = score(
        (raw_p0, raw_p1, raw_p2, raw_p3), (raw_q0, raw_q1, raw_q2, raw_q3), chosen, valid
    )

    spread = (
        block_of.reshape(ranks, CAP, 1, per_block)
        == lax.broadcasted_iota(jnp.int32, (1, 1, blocks, 1), 2)
    ).astype(F32)
    both = jnp.concatenate([sums, hits], axis=0).reshape(2, ranks, CAP, 1, per_block)
    both = jnp.sum(both * spread[None], axis=2)
    packed = both.reshape(-1, blocks * per_block)
    packed = ring_sum(packed, first)
    packed = ring_sum(packed, second)
    packed = packed + swap(packed)
    packed = ring_sum(packed, third)
    both = packed.reshape(2, ranks, blocks, per_block)
    losses = (jnp.log(both[0]) - both[1]).reshape(-1)
    out_share = queries // groups
    loss_out = lax.dynamic_slice_in_dim(losses, (dp * groups + column) * out_share, out_share, 0)
    denom = jnp.sum(both[0][:, None] * spread, axis=2).reshape(1, rows)
    denom = jnp.where(valid == 1, denom, 1.0)
    d_mine, d_theirs = backward(emb, exps, scale, denom, chosen)

    d_other = swap(d_theirs)
    states = (passage_last_states, asked, other_states, other_asked)
    part = depth // SIDE
    terms = functools.partial(weight_terms, states, d_mine, d_other, u, part=part)
    far0, far1 = terms(items=[(2, 0), (2, 1)])
    from_left = first(far0, 1)
    from_right = first(far1, -1)
    right1, left0 = terms(items=[(1, 1), (3, 0)])
    left1_in = first(right1, 1)
    right0_in = first(left0, -1)
    right0, left1 = terms(items=[(1, 0), (3, 1)], added=(from_left, from_right))
    left0_in = first(right0, 1)
    right1_in = first(left1, -1)
    (summed,) = terms(items=[(0, 0), (0, 1)], added=(right0_in, left1_in), joined=True)
    summed = add(summed, jnp.concatenate([left0_in, right1_in], axis=0))

    part2 = part // SIDE

    def chunk(step):
        return lax.dynamic_slice_in_dim(summed, lax.rem(v + step, SIDE) * part2, part2, 0)

    summed = add(
        chunk(0), second(chunk(1), 1), second(chunk(3), -1), second(chunk(2), 2)
    )
    cols = [summed[:, step * half : (step + 1) * half] for step in range(SIDE)]
    piece = add(cols[0], third(cols[1], 1), third(cols[3], -1), third(cols[2], 2))

    piece = jnp.concatenate(
        [piece, second(piece, -1), second(piece, 2), second(piece, 1)], axis=0
    )
    middle = piece.shape[0] // 2
    left = first(piece, 1)
    right = first(piece, -1)
    mine = [piece, right, first(left[:middle], 1), first(right[middle:], -1), left]
    other = [swap(block) for block in mine]
    return (loss_out, place_all(mine, other, u, v, core))


def solution(mesh):
    return jax.shard_map(
        shards,
        mesh=mesh,
        in_specs=(
            P("dp", None),
            P(("dp", "psg"), None),
            P(None, "psg"),
            P(None, "dp", None),
            P("dp"),
        ),
        out_specs=(P(("dp", "psg")), P(None, "psg")),
        check_vma=False,
    )
```

```python
import functools

import jax
import jax.numpy as jnp
from jax import lax
from jax.experimental import pallas as pl
from jax.experimental.pallas import tpu as pltpu
from jax.sharding import PartitionSpec as P

CAP = 2
INV_TAU = 50.0
F32 = jnp.float32
BF16 = jnp.bfloat16
SIDE = 4
COVER = 6.0


def dp_perm(move):
    pairs = []
    for x in range(SIDE):
        for y in range(SIDE):
            for core in range(2):
                tx, ty, tcore = move(x, y, core)
                target = ((tx % SIDE) * SIDE + ty % SIDE) * 2 + tcore
                pairs.append(((x * SIDE + y) * 2 + core, target))
    return pairs


def first(value, step):
    return lax.ppermute(
        value, "dp", dp_perm(lambda x, y, k: (x + step, y, k) if k == 0 else (x, y + step, k))
    )


def second(value, step):
    return lax.ppermute(
        value, "dp", dp_perm(lambda x, y, k: (x, y + step, k) if k == 0 else (x + step, y, k))
    )


def third(value, step):
    return lax.ppermute(value, "psg", [(c, (c + step) % SIDE) for c in range(SIDE)])


def swap(value):
    return lax.ppermute(value, "dp", dp_perm(lambda x, y, k: (x, y, 1 - k)))


def ring_sum(value, move):
    return value + move(value, 1) + move(value, -1) + move(value, 2)


def dot(left, right, contract):
    return lax.dot_general(
        left, right, ((contract[:1], contract[1:]), ((), ())), preferred_element_type=F32
    )


def limit(mebibytes):
    return pltpu.CompilerParams(vmem_limit_bytes=mebibytes * 2**20)


def in_hbm(value):
    return pltpu.with_memory_space_constraint(value, pltpu.HBM)


def cost(flops, nbytes, exps=0):
    return pl.CostEstimate(flops=flops, bytes_accessed=nbytes, transcendentals=exps)


def project_kernel(sets, _, *refs):
    outs = refs[-sets[0] * sets[1] :]
    states = refs[: sets[0]]
    weights = refs[sets[0] : len(refs) - len(outs)]
    deep, half = weights[0].shape
    for i, state in enumerate(states):
        for j in range(sets[1]):
            out = outs[i * sets[1] + j]
            for col in range(2):
                top, bottom = weights[4 * j + 2 * col : 4 * j + 2 * col + 2]
                out[:, col * half : (col + 1) * half] = dot(
                    state[:, :deep], top[...], (1, 0)
                ) + dot(state[:, deep : 2 * deep], bottom[...], (1, 0))


def project(states, quarters, core, memory, weight=1.0, kept=False):
    rows = states[0].shape[0]
    weights = []
    specs = []
    for quarter in quarters:
        for side in range(2):
            for i in range(2):
                if isinstance(quarter, list):
                    weights.append(quarter[side][i])
                    deep, half = weights[-1].shape
                    place = lambda _, core: (0, 0)
                else:
                    weights.append(quarter)
                    deep, half = quarter.shape[0] // 2, quarter.shape[1] // 2
                    place = lambda _, core, i=i, side=side: (i, core[side])
                specs.append(pl.BlockSpec((deep, half), place, pipeline_mode=pl.Buffered(1)))
    steps = 2
    state = pl.BlockSpec((rows // steps, 2 * deep), lambda i, core: (i, 0))
    out = pl.BlockSpec((rows // steps, 2 * half), lambda i, core: (i, 0))
    count = len(states) * len(quarters)
    return pl.pallas_call(
        functools.partial(project_kernel, (len(states), len(quarters))),
        grid_spec=pltpu.PrefetchScalarGridSpec(
            num_scalar_prefetch=1,
            grid=(steps,),
            in_specs=[state] * len(states) + specs,
            out_specs=[out] * count,
        ),
        out_shape=[(jax.ShapeDtypeStruct if kept else pltpu.HBM)((rows, 2 * half), F32)] * count,
        compiler_params=limit(memory),
        cost_estimate=cost(
            int(weight * 8 * rows * deep * half * count),
            4 * rows * deep * len(states) + 8 * deep * half * len(quarters),
        ),
        name="project",
    )(core, *map(in_hbm, states), *map(in_hbm, weights))


def score_kernel(*refs):
    raw_p, raw_q = refs[:SIDE], refs[SIDE : 2 * SIDE]
    chosen, valid, emb_out, exps, scale_out, sums, hits, emb = refs[2 * SIDE :]
    step = pl.program_id(0)
    tile, width = raw_p[0].shape
    rows = exps.shape[0]

    def normalise(raws):
        values = [raw[...] for raw in raws]
        square = values[0] * values[0]
        for value in values[1:]:
            square = square + value * value
        scale = 1.0 / jnp.sqrt(jnp.sum(square, axis=1, keepdims=True) + 1e-06)
        scale_out[...] = scale
        for i, value in enumerate(values):
            rounded = (value * scale).astype(BF16)
            emb[pl.ds(pl.multiple_of(step * tile, tile), tile), i * width : (i + 1) * width] = rounded
            emb_out[:, i * width : (i + 1) * width] = rounded

    @pl.when(step < rows // tile)
    def _():
        normalise(raw_p)

    @pl.when(step >= rows // tile)
    def _():
        normalise(raw_q)

    @pl.when(step == pl.num_programs(0) - 1)
    def _():
        chunk = rows // SIDE
        queries = emb[rows:, :]
        total = jnp.zeros((1, queries.shape[0]), F32)
        found = jnp.zeros((1, queries.shape[0]), F32)
        for i in range(SIDE):
            part = dot(emb[i * chunk : (i + 1) * chunk, :], queries, (1, 1)) * INV_TAU
            place = lax.broadcasted_iota(jnp.int32, part.shape, 0) + i * chunk
            value = jnp.exp(part)
            exps[i * chunk : (i + 1) * chunk, :] = value
            total = total + jnp.sum(value, axis=0, keepdims=True)
            found = found + jnp.sum(
                jnp.where(place == chosen[...], part, 0.0), axis=0, keepdims=True
            )
        sums[...] = jnp.where(valid[...] == 1, total, 0.0)
        hits[...] = found


def score(raws, raws_q, chosen, valid):
    rows, width = raws[0].shape
    both = 2 * rows
    steps = 8
    tile = both // steps
    features = width * SIDE
    raw_p = pl.BlockSpec((tile, width), lambda i: (jnp.minimum(i, rows // tile - 1), 0))
    raw_q = pl.BlockSpec((tile, width), lambda i: (jnp.maximum(i - rows // tile, 0), 0))
    line = pl.BlockSpec((1, rows), lambda i: (0, 0))
    return pl.pallas_call(
        score_kernel,
        grid=(steps,),
        in_specs=[raw_p] * SIDE + [raw_q] * SIDE + [line] * 2,
        out_specs=[
            pl.BlockSpec((tile, features), lambda i: (i, 0)),
            pl.BlockSpec((rows, rows), lambda i: (0, 0)),
            pl.BlockSpec((tile, 1), lambda i: (i, 0)),
            line,
            line,
        ],
        out_shape=[
            jax.ShapeDtypeStruct((both, features), BF16),
            jax.ShapeDtypeStruct((rows, rows), F32),
            jax.ShapeDtypeStruct((both, 1), F32),
            jax.ShapeDtypeStruct((1, rows), F32),
            jax.ShapeDtypeStruct((1, rows), F32),
        ],
        scratch_shapes=[pltpu.VMEM((both, features), BF16)],
        compiler_params=limit(15),
        cost_estimate=cost(2 * rows * rows * features, 6 * both * features + 4 * rows * rows, rows * rows),
        name="score",
    )(*raws, *raws_q, chosen, valid)


def backward_kernel(
    source, exps, scale, denom, chosen, mine_out, theirs_out, emb, grads, d_emb, mine, theirs, sems, out_sems
):
    rows = exps.shape[0]
    features = emb.shape[1]
    width = features // SIDE
    half = width // 2
    loads = [
        pltpu.make_async_copy(
            source.at[pl.ds(kind * rows, rows), :], emb.at[pl.ds(kind * rows, rows), :], sems.at[kind]
        )
        for kind in range(2)
    ]
    loads[1].start()
    loads[0].start()
    inverse = 1.0 / denom[...]
    chunk = rows // SIDE
    for i in range(SIDE):
        where = slice(i * chunk, (i + 1) * chunk)
        place = lax.broadcasted_iota(jnp.int32, (chunk, rows), 0) + i * chunk
        target = jnp.where(place == chosen[...], 1.0, 0.0)
        grads[where, :] = (exps[where, :] * inverse - target).astype(BF16)
    loads[1].wait()
    for i in range(SIDE):
        cols = slice(i * width, (i + 1) * width)
        d_emb[:rows, cols] = dot(grads[...], emb[rows:, cols], (1, 0)) * INV_TAU
    loads[0].wait()
    for i in range(SIDE):
        cols = slice(i * width, (i + 1) * width)
        d_emb[rows:, cols] = dot(grads[...], emb[:rows, cols], (0, 0)) * INV_TAU
    tile = 64
    part = 2 * rows // SIDE
    sent = []
    for block in range(SIDE):

        @pl.loop(block * part // tile, (block + 1) * part // tile)
        def _(step):
            where = pl.ds(pl.multiple_of(step * tile, tile), tile)
            inner = jnp.zeros((tile, 1), F32)
            for i in range(SIDE):
                cols = slice(i * width, (i + 1) * width)
                inner = inner + jnp.sum(
                    emb[where, cols].astype(F32) * d_emb[where, cols], axis=1, keepdims=True
                )
            factor = scale[where, :]
            for i in range(SIDE):
                for j, out in enumerate((mine, theirs)):
                    cols = slice(i * width + j * half, i * width + (j + 1) * half)
                    out[where, i * half : (i + 1) * half] = (
                        (d_emb[where, cols] - emb[where, cols].astype(F32) * inner) * factor
                    ).astype(BF16)

        span = pl.ds(block * part, part)
        for held, out in ((theirs, theirs_out), (mine, mine_out)):
            sent.append(
                pltpu.make_async_copy(held.at[span, :], out.at[span, :], out_sems.at[len(sent)])
            )
            sent[-1].start()
    for copy in sent:
        copy.wait()


def backward(emb, exps, scale, denom, chosen):
    both, features = emb.shape
    rows = both // 2
    anywhere = pl.BlockSpec(memory_space=pl.ANY)
    return pl.pallas_call(
        backward_kernel,
        in_specs=[anywhere] + [pl.BlockSpec(memory_space=pltpu.VMEM)] * 4,
        out_specs=[anywhere] * 2,
        out_shape=[jax.ShapeDtypeStruct((both, features // 2), BF16)] * 2,
        scratch_shapes=[
            pltpu.VMEM((both, features), BF16),
            pltpu.VMEM((rows, rows), BF16),
            pltpu.VMEM((both, features), F32),
            pltpu.VMEM((both, features // 2), BF16),
            pltpu.VMEM((both, features // 2), BF16),
            pltpu.SemaphoreType.DMA((2,)),
            pltpu.SemaphoreType.DMA((2 * SIDE,)),
        ],
        compiler_params=limit(22),
        cost_estimate=cost(4 * rows * rows * features, 4 * both * features + 4 * rows * rows),
        name="backward",
    )(emb, exps, scale, denom, chosen)


ITEMS = 2


def weight_kernel(joined, cols, p, q, op, oq, d, od, *refs):
    del cols
    step = pl.program_id(0)
    held, grads, extra, out_sems, in_sems = refs[-5:]
    outs = refs[-6:-5] if joined else refs[-5 - ITEMS : -5]
    added = refs[: len(refs) - 5 - len(outs)]
    tile = held.shape[1]
    rows = p.shape[0]
    states = (p, q, op, oq)
    copies = []
    for i, source in enumerate((d, od)):
        for j in range(2):
            number = len(copies)
            copies.append(
                pltpu.make_async_copy(
                    source.at[pl.ds(j * rows, rows), :], grads.at[number], in_sems.at[number]
                )
            )
    for i, source in enumerate(added):
        copies.append(
            pltpu.make_async_copy(source, extra.at[i], in_sems.at[len(states) + i])
        )
    sent = [
        pltpu.make_async_copy(
            held.at[i],
            outs[0].at[pl.ds(i * tile, tile), :] if joined else outs[i],
            out_sems.at[i],
        )
        for i in range(ITEMS)
    ]
    first_step = step == 0

    @pl.when(first_step)
    def _():
        for copy in copies:
            copy.start()

    value = None
    for i, state in enumerate(states):

        @pl.when(first_step)
        def _():
            copies[i].wait()

        term = dot(state[...], grads[i], (0, 0))
        value = term if value is None else value + term
    for i in range(ITEMS):

        @pl.when(step == i)
        def _():
            total = value
            if added:
                copies[len(states) + i].wait()
                total = value + extra[i].astype(F32)
            held[i] = total.astype(BF16)
            sent[i].start()

    @pl.when(step == ITEMS - 1)
    def _():
        for copy in sent:
            copy.wait()


def weight_terms(states, d_mine, d_other, u, items, part, added=(), joined=False):
    rows = states[0].shape[0]
    tile = part // 2
    keep = d_mine.shape[1]
    count = len(items)
    cols = jnp.stack([lax.rem(u + step, SIDE) * 2 + half for step, half in items])
    state = pl.BlockSpec((rows, tile), lambda i, cols: (0, cols[i]))
    anywhere = pl.BlockSpec(memory_space=pl.ANY)
    shapes = [(count * tile, keep)] if joined else [(tile, keep)] * count
    return pl.pallas_call(
        functools.partial(weight_kernel, joined),
        grid_spec=pltpu.PrefetchScalarGridSpec(
            num_scalar_prefetch=1,
            grid=(count,),
            in_specs=[state] * 4 + [anywhere] * (2 + len(added)),
            out_specs=[anywhere] * len(shapes),
            scratch_shapes=[
                pltpu.VMEM((count, tile, keep), BF16),
                pltpu.VMEM((4, rows, keep), BF16),
                pltpu.VMEM((max(1, len(added)), tile, keep), BF16),
                pltpu.SemaphoreType.DMA((count,)),
                pltpu.SemaphoreType.DMA((4 + count,)),
            ],
        ),
        out_shape=[jax.ShapeDtypeStruct(shape, BF16) for shape in shapes],
        compiler_params=limit(20),
        cost_estimate=cost(
            2 * rows * tile * keep * count, (2 * rows * tile + tile * keep) * count
        ),
        name="weight_terms",
    )(cols.astype(jnp.int32), *states, d_mine, d_other, *added)


def place_kernel(places, *refs):
    *pieces, out = refs
    count = len(pieces) // 2
    half = pieces[0].shape[1]
    rows = out.shape[0] // (SIDE * SIDE)
    core = places[2]
    for side in range(2):
        a = places[side]
        b = places[1 - side]

        def fill(column, side=side, a=a, b=b):
            for number in range(count):
                ref = pieces[side * count + number]
                for inner in range(ref.shape[0] // rows):
                    far = (0, 1, 2, 2, 3)[number]
                    rel = inner + (2 if number == 3 else 0)
                    row = lax.rem(a + far, SIDE) * SIDE + lax.rem(b + rel, SIDE)
                    out[pl.ds(pl.multiple_of(row * rows, rows), rows), column * half : (column + 1) * half] = (
                        ref[inner * rows : (inner + 1) * rows, :]
                    )

        @pl.when(core == 0)
        def _():
            fill(side)

        @pl.when(core != 0)
        def _():
            fill(1 - side)


def place_all(mine, other, u, v, core):
    total = SIDE * SIDE * (mine[0].shape[0] // SIDE)
    half = mine[0].shape[1]
    places = jnp.stack([u, v, core]).astype(jnp.int32)
    return pl.pallas_call(
        place_kernel,
        in_specs=[pl.BlockSpec(memory_space=pltpu.SMEM)] + [pl.BlockSpec(memory_space=pltpu.VMEM)] * 10,
        out_specs=pl.BlockSpec(memory_space=pltpu.VMEM),
        out_shape=jax.ShapeDtypeStruct((total, 2 * half), BF16),
        compiler_params=limit(10),
        name="place_all",
    )(places, *mine, *other)


def add(*values):
    total = values[0].astype(F32)
    for value in values[1:]:
        total = total + value.astype(F32)
    return total.astype(BF16)


def lines_of(mine, per_block):
    blocks, _ = mine.shape
    same = (mine[:, :, None, None] == mine[None, None, :, :]).astype(jnp.int32)
    before = (
        lax.broadcasted_iota(jnp.int32, (blocks, blocks), 1)
        < lax.broadcasted_iota(jnp.int32, (blocks, blocks), 0)
    ).astype(jnp.int32)
    place = jnp.sum(same * before[:, None, :, None], axis=(2, 3))
    return jnp.repeat((mine * CAP + place).T, per_block, axis=1)


def route_kernel(per_block, lines, states, facts, lead_facts, out):
    tile = out.shape[0]
    queries, depth = states.shape
    row = lax.broadcasted_iota(jnp.int32, (tile, queries), 0) + pl.program_id(0) * tile
    col = lax.broadcasted_iota(jnp.int32, (tile, queries), 1)
    aligned = jnp.bitwise_and(row, per_block - 1) == jnp.bitwise_and(col, per_block - 1)
    line = jnp.right_shift(row, per_block.bit_length() - 1)
    lead = aligned & (line == lines[0:1, :])
    both = lead | (aligned & (line == lines[1:2, :]))
    lead = jnp.where(lead, 1.0, 0.0).astype(BF16)
    both = jnp.where(both, 1.0, 0.0).astype(BF16)
    out[:, :depth] = dot(both, states[...], (1, 0)).astype(BF16)
    out[:, depth:] = (
        dot(both, facts[...], (1, 0)) + dot(lead, lead_facts[...], (1, 0))
    ).astype(BF16)


def route(lines, states, facts, lead_facts, rows, per_block):
    queries, depth = states.shape
    steps = 4
    wide = depth + facts.shape[1]

    def whole(value):
        return pl.BlockSpec(value.shape, lambda i: (0, 0))

    return pl.pallas_call(
        functools.partial(route_kernel, per_block),
        grid=(steps,),
        in_specs=[whole(value) for value in (lines, states, facts, lead_facts)],
        out_specs=pl.BlockSpec((rows // steps, wide), lambda i: (i, 0)),
        out_shape=pltpu.HBM((rows, wide), BF16),
        compiler_params=limit(10),
        cost_estimate=cost(2 * rows * queries * wide, 2 * (rows + queries) * wide),
        name="route",
    )(lines, states, facts, lead_facts)


def shards(query_states, passage_last_states, head_weight, negatives, positives):
    ranks = lax.axis_size("dp")
    groups = lax.axis_size("psg")
    dp = lax.axis_index("dp")
    column = lax.axis_index("psg")
    core = lax.rem(dp, 2)
    x = dp // (2 * SIDE)
    y = lax.rem(dp // 2, SIDE)
    u = jnp.where(core == 0, x, y)
    v = jnp.where(core == 0, y, x)
    queries, depth = query_states.shape
    blocks = negatives.shape[1]
    per_block = queries // blocks
    share = head_weight.shape[1]
    half = share // 2
    deep = depth // 2

    def own(row):
        return lax.dynamic_slice(head_weight, (row * deep, core * half), (deep, half))

    top, bottom, query_states = lax.optimization_barrier((own(0), own(1), query_states))
    left_top = third(top, 1)
    right_bottom = third(bottom, -1)
    left_bottom = third(bottom, 1)
    right_top = third(top, -1)
    sides = jnp.stack([core, 1 - core]).astype(jnp.int32)
    (raw_p0,) = project([passage_last_states], [head_weight], sides, 12)
    left_top, left_bottom, right_top, right_bottom, raw_p0 = lax.optimization_barrier(
        (left_top, left_bottom, right_top, right_bottom, raw_p0)
    )
    mine1 = [right_top, right_bottom]
    mine3 = [left_top, left_bottom]
    theirs1 = [swap(piece) for piece in mine1]
    theirs3 = [swap(piece) for piece in mine3]
    mine2 = [third(left_top, 1), third(right_bottom, -1)]

    picked = lax.dynamic_index_in_dim(negatives, column, 0, keepdims=False)
    lines = lines_of(picked, per_block)
    number = lax.broadcasted_iota(jnp.int32, (queries, 1), 0) // per_block
    facts = jnp.concatenate(
        [jnp.ones_like(number), number, positives[:, None] // 16, positives[:, None] % 16], axis=1
    ).astype(BF16)
    facts = jnp.pad(facts, ((0, 0), (0, 128 - facts.shape[1])))
    lead_facts = (
        (lax.broadcasted_iota(jnp.int32, facts.shape, 1) == 4) & (column == 0)
    ).astype(BF16)
    rows = ranks * CAP * per_block
    outgoing = route(lines, query_states, facts, lead_facts, rows, per_block)
    asked = lax.all_to_all(
        outgoing.reshape(ranks, rows // ranks, depth + 128),
        "dp",
        split_axis=0,
        concat_axis=0,
        tiled=True,
    ).reshape(rows, depth + 128)
    facts = asked[:, depth : depth + 8].astype(jnp.int32).T
    valid = facts[0:1]
    block_of = facts[1]
    chosen = jnp.where(facts[4:5] == 1, facts[2:3] * 16 + facts[3:4], -1)

    other_states = swap(passage_last_states)
    other_asked = swap(asked)

    near = [[mine1, theirs1], [mine3, theirs3]]
    raw_p1, raw_p3 = project([passage_last_states], near, sides, 17, COVER)
    asked, raw_p0, raw_p1, raw_p3 = lax.optimization_barrier((asked, raw_p0, raw_p1, raw_p3))
    raw_q0, raw_q1, raw_q3 = project([asked], [head_weight, *near], sides, 22)
    *mine2, raw_q0, raw_q1, raw_q3 = lax.optimization_barrier((*mine2, raw_q0, raw_q1, raw_q3))
    theirs2 = [swap(piece) for piece in mine2]
    raw_p2, raw_q2 = project([passage_last_states, asked], [[mine2, theirs2]], sides, 17, kept=True)
    emb, exps, scale, sums, hits = score(
        (raw_p0, raw_p1, raw_p2, raw_p3), (raw_q0, raw_q1, raw_q2, raw_q3), chosen, valid
    )

    spread = (
        block_of.reshape(ranks, CAP, 1, per_block)
        == lax.broadcasted_iota(jnp.int32, (1, 1, blocks, 1), 2)
    ).astype(F32)
    both = jnp.concatenate([sums, hits], axis=0).reshape(2, ranks, CAP, 1, per_block)
    both = jnp.sum(both * spread[None], axis=2)
    packed = both.reshape(-1, blocks * per_block)
    packed = ring_sum(packed, first)
    packed = ring_sum(packed, second)
    packed = packed + swap(packed)
    packed = ring_sum(packed, third)
    both = packed.reshape(2, ranks, blocks, per_block)
    losses = (jnp.log(both[0]) - both[1]).reshape(-1)
    out_share = queries // groups
    loss_out = lax.dynamic_slice_in_dim(losses, (dp * groups + column) * out_share, out_share, 0)
    denom = jnp.sum(both[0][:, None] * spread, axis=2).reshape(1, rows)
    denom = jnp.where(valid == 1, denom, 1.0)
    d_mine, d_theirs = backward(emb, exps, scale, denom, chosen)

    d_other = swap(d_theirs)
    states = (passage_last_states, asked, other_states, other_asked)
    part = depth // SIDE
    terms = functools.partial(weight_terms, states, d_mine, d_other, u, part=part)
    far0, far1 = terms(items=[(2, 0), (2, 1)])
    from_left = first(far0, 1)
    from_right = first(far1, -1)
    right1, left0 = terms(items=[(1, 1), (3, 0)])
    left1_in = first(right1, 1)
    right0_in = first(left0, -1)
    right0, left1 = terms(items=[(1, 0), (3, 1)], added=(from_left, from_right))
    left0_in = first(right0, 1)
    right1_in = first(left1, -1)
    (summed,) = terms(items=[(0, 0), (0, 1)], added=(right0_in, left1_in), joined=True)
    summed = add(summed, jnp.concatenate([left0_in, right1_in], axis=0))

    part2 = part // SIDE

    def chunk(step):
        return lax.dynamic_slice_in_dim(summed, lax.rem(v + step, SIDE) * part2, part2, 0)

    summed = add(
        chunk(0), second(chunk(1), 1), second(chunk(3), -1), second(chunk(2), 2)
    )
    cols = [summed[:, step * half : (step + 1) * half] for step in range(SIDE)]
    piece = add(cols[0], third(cols[1], 1), third(cols[3], -1), third(cols[2], 2))

    piece = jnp.concatenate(
        [piece, second(piece, -1), second(piece, 2), second(piece, 1)], axis=0
    )
    middle = piece.shape[0] // 2
    left = first(piece, 1)
    right = first(piece, -1)
    mine = [piece, right, first(left[:middle], 1), first(right[middle:], -1), left]
    other = [swap(block) for block in mine]
    return (loss_out, place_all(mine, other, u, v, core))


def solution(mesh):
    return jax.shard_map(
        shards,
        mesh=mesh,
        in_specs=(
            P("dp", None),
            P(("dp", "psg"), None),
            P(None, "psg"),
            P(None, "dp", None),
            P("dp"),
        ),
        out_specs=(P(("dp", "psg")), P(None, "psg")),
        check_vma=False,
    )
```

```python
import functools

import jax
import jax.numpy as jnp
from jax import lax
from jax.experimental import pallas as pl
from jax.experimental.pallas import tpu as pltpu
from jax.sharding import PartitionSpec as P

CAP = 2
INV_TAU = 50.0
F32 = jnp.float32
BF16 = jnp.bfloat16
SIDE = 4
COVER = 6.0


def dp_perm(move):
    pairs = []
    for x in range(SIDE):
        for y in range(SIDE):
            for core in range(2):
                tx, ty, tcore = move(x, y, core)
                target = ((tx % SIDE) * SIDE + ty % SIDE) * 2 + tcore
                pairs.append(((x * SIDE + y) * 2 + core, target))
    return pairs


def first(value, step):
    return lax.ppermute(
        value, "dp", dp_perm(lambda x, y, k: (x + step, y, k) if k == 0 else (x, y + step, k))
    )


def second(value, step):
    return lax.ppermute(
        value, "dp", dp_perm(lambda x, y, k: (x, y + step, k) if k == 0 else (x + step, y, k))
    )


def third(value, step):
    return lax.ppermute(value, "psg", [(c, (c + step) % SIDE) for c in range(SIDE)])


def swap(value):
    return lax.ppermute(value, "dp", dp_perm(lambda x, y, k: (x, y, 1 - k)))


def ring_sum(value, move):
    return value + move(value, 1) + move(value, -1) + move(value, 2)


def dot(left, right, contract):
    return lax.dot_general(
        left, right, ((contract[:1], contract[1:]), ((), ())), preferred_element_type=F32
    )


def limit(mebibytes):
    return pltpu.CompilerParams(vmem_limit_bytes=mebibytes * 2**20)


def in_hbm(value):
    return pltpu.with_memory_space_constraint(value, pltpu.HBM)


def cost(flops, nbytes, exps=0):
    return pl.CostEstimate(flops=flops, bytes_accessed=nbytes, transcendentals=exps)


def project_kernel(sets, _, *refs):
    outs = refs[-sets[0] * sets[1] :]
    states = refs[: sets[0]]
    weights = refs[sets[0] : len(refs) - len(outs)]
    deep, half = weights[0].shape
    for i, state in enumerate(states):
        for j in range(sets[1]):
            out = outs[i * sets[1] + j]
            for col in range(2):
                top, bottom = weights[4 * j + 2 * col : 4 * j + 2 * col + 2]
                out[:, col * half : (col + 1) * half] = dot(
                    state[:, :deep], top[...], (1, 0)
                ) + dot(state[:, deep : 2 * deep], bottom[...], (1, 0))


def project(states, quarters, core, memory, weight=1.0, kept=False):
    rows = states[0].shape[0]
    weights = []
    specs = []
    for quarter in quarters:
        for side in range(2):
            for i in range(2):
                if isinstance(quarter, list):
                    weights.append(quarter[side][i])
                    deep, half = weights[-1].shape
                    place = lambda _, core: (0, 0)
                else:
                    weights.append(quarter)
                    deep, half = quarter.shape[0] // 2, quarter.shape[1] // 2
                    place = lambda _, core, i=i, side=side: (i, core[side])
                specs.append(pl.BlockSpec((deep, half), place, pipeline_mode=pl.Buffered(1)))
    steps = 2
    state = pl.BlockSpec((rows // steps, 2 * deep), lambda i, core: (i, 0))
    out = pl.BlockSpec((rows // steps, 2 * half), lambda i, core: (i, 0))
    count = len(states) * len(quarters)
    return pl.pallas_call(
        functools.partial(project_kernel, (len(states), len(quarters))),
        grid_spec=pltpu.PrefetchScalarGridSpec(
            num_scalar_prefetch=1,
            grid=(steps,),
            in_specs=[state] * len(states) + specs,
            out_specs=[out] * count,
        ),
        out_shape=[(jax.ShapeDtypeStruct if kept else pltpu.HBM)((rows, 2 * half), F32)] * count,
        compiler_params=limit(memory),
        cost_estimate=cost(
            int(weight * 8 * rows * deep * half * count),
            4 * rows * deep * len(states) + 8 * deep * half * len(quarters),
        ),
        name="project",
    )(core, *map(in_hbm, states), *map(in_hbm, weights))


def score_kernel(*refs):
    raw_p, raw_q = refs[:SIDE], refs[SIDE : 2 * SIDE]
    chosen, valid, emb_out, exps, scale_out, sums, hits, emb = refs[2 * SIDE :]
    step = pl.program_id(0)
    tile, width = raw_p[0].shape
    rows = exps.shape[0]

    def normalise(raws):
        values = [raw[...] for raw in raws]
        square = values[0] * values[0]
        for value in values[1:]:
            square = square + value * value
        scale = 1.0 / jnp.sqrt(jnp.sum(square, axis=1, keepdims=True) + 1e-06)
        scale_out[...] = scale
        for i, value in enumerate(values):
            rounded = (value * scale).astype(BF16)
            emb[pl.ds(pl.multiple_of(step * tile, tile), tile), i * width : (i + 1) * width] = rounded
            emb_out[:, i * width : (i + 1) * width] = rounded

    @pl.when(step < rows // tile)
    def _():
        normalise(raw_p)

    @pl.when(step >= rows // tile)
    def _():
        normalise(raw_q)

    @pl.when(step == pl.num_programs(0) - 1)
    def _():
        chunk = rows // SIDE
        queries = emb[rows:, :]
        total = jnp.zeros((1, queries.shape[0]), F32)
        found = jnp.zeros((1, queries.shape[0]), F32)
        for i in range(SIDE):
            part = dot(emb[i * chunk : (i + 1) * chunk, :], queries, (1, 1)) * INV_TAU
            place = lax.broadcasted_iota(jnp.int32, part.shape, 0) + i * chunk
            value = jnp.exp(part)
            exps[i * chunk : (i + 1) * chunk, :] = value
            total = total + jnp.sum(value, axis=0, keepdims=True)
            found = found + jnp.sum(
                jnp.where(place == chosen[...], part, 0.0), axis=0, keepdims=True
            )
        sums[...] = jnp.where(valid[...] == 1, total, 0.0)
        hits[...] = found


def score(raws, raws_q, chosen, valid):
    rows, width = raws[0].shape
    both = 2 * rows
    steps = 8
    tile = both // steps
    features = width * SIDE
    raw_p = pl.BlockSpec((tile, width), lambda i: (jnp.minimum(i, rows // tile - 1), 0))
    raw_q = pl.BlockSpec((tile, width), lambda i: (jnp.maximum(i - rows // tile, 0), 0))
    line = pl.BlockSpec((1, rows), lambda i: (0, 0))
    return pl.pallas_call(
        score_kernel,
        grid=(steps,),
        in_specs=[raw_p] * SIDE + [raw_q] * SIDE + [line] * 2,
        out_specs=[
            pl.BlockSpec((tile, features), lambda i: (i, 0)),
            pl.BlockSpec((rows, rows), lambda i: (0, 0)),
            pl.BlockSpec((tile, 1), lambda i: (i, 0)),
            line,
            line,
        ],
        out_shape=[
            jax.ShapeDtypeStruct((both, features), BF16),
            jax.ShapeDtypeStruct((rows, rows), F32),
            pltpu.HBM((both, 1), F32),
            jax.ShapeDtypeStruct((1, rows), F32),
            jax.ShapeDtypeStruct((1, rows), F32),
        ],
        scratch_shapes=[pltpu.VMEM((both, features), BF16)],
        compiler_params=limit(15),
        cost_estimate=cost(2 * rows * rows * features, 6 * both * features + 4 * rows * rows, rows * rows),
        name="score",
    )(*raws, *raws_q, chosen, valid)


def backward_kernel(
    source, exps, scale, denom, chosen, mine_out, theirs_out, emb, grads, d_emb, mine, theirs, sems, out_sems
):
    rows = exps.shape[0]
    features = emb.shape[1]
    width = features // SIDE
    half = width // 2
    loads = [
        pltpu.make_async_copy(
            source.at[pl.ds(kind * rows, rows), :], emb.at[pl.ds(kind * rows, rows), :], sems.at[kind]
        )
        for kind in range(2)
    ]
    loads[1].start()
    loads[0].start()
    inverse = 1.0 / denom[...]
    chunk = rows // SIDE
    for i in range(SIDE):
        where = slice(i * chunk, (i + 1) * chunk)
        place = lax.broadcasted_iota(jnp.int32, (chunk, rows), 0) + i * chunk
        target = jnp.where(place == chosen[...], 1.0, 0.0)
        grads[where, :] = (exps[where, :] * inverse - target).astype(BF16)
    loads[1].wait()
    for i in range(SIDE):
        cols = slice(i * width, (i + 1) * width)
        d_emb[:rows, cols] = dot(grads[...], emb[rows:, cols], (1, 0)) * INV_TAU
    loads[0].wait()
    for i in range(SIDE):
        cols = slice(i * width, (i + 1) * width)
        d_emb[rows:, cols] = dot(grads[...], emb[:rows, cols], (0, 0)) * INV_TAU
    tile = 64
    part = 2 * rows // SIDE
    sent = []
    for block in range(SIDE):

        @pl.loop(block * part // tile, (block + 1) * part // tile)
        def _(step):
            where = pl.ds(pl.multiple_of(step * tile, tile), tile)
            inner = jnp.zeros((tile, 1), F32)
            for i in range(SIDE):
                cols = slice(i * width, (i + 1) * width)
                inner = inner + jnp.sum(
                    emb[where, cols].astype(F32) * d_emb[where, cols], axis=1, keepdims=True
                )
            factor = scale[where, :]
            for i in range(SIDE):
                for j, out in enumerate((mine, theirs)):
                    cols = slice(i * width + j * half, i * width + (j + 1) * half)
                    out[where, i * half : (i + 1) * half] = (
                        (d_emb[where, cols] - emb[where, cols].astype(F32) * inner) * factor
                    ).astype(BF16)

        span = pl.ds(block * part, part)
        for held, out in ((theirs, theirs_out), (mine, mine_out)):
            sent.append(
                pltpu.make_async_copy(held.at[span, :], out.at[span, :], out_sems.at[len(sent)])
            )
            sent[-1].start()
    for copy in sent:
        copy.wait()


def backward(emb, exps, scale, denom, chosen):
    both, features = emb.shape
    rows = both // 2
    anywhere = pl.BlockSpec(memory_space=pl.ANY)
    return pl.pallas_call(
        backward_kernel,
        in_specs=[anywhere] + [pl.BlockSpec(memory_space=pltpu.VMEM)] * 4,
        out_specs=[anywhere] * 2,
        out_shape=[jax.ShapeDtypeStruct((both, features // 2), BF16)] * 2,
        scratch_shapes=[
            pltpu.VMEM((both, features), BF16),
            pltpu.VMEM((rows, rows), BF16),
            pltpu.VMEM((both, features), F32),
            pltpu.VMEM((both, features // 2), BF16),
            pltpu.VMEM((both, features // 2), BF16),
            pltpu.SemaphoreType.DMA((2,)),
            pltpu.SemaphoreType.DMA((2 * SIDE,)),
        ],
        compiler_params=limit(22),
        cost_estimate=cost(4 * rows * rows * features, 4 * both * features + 4 * rows * rows),
        name="backward",
    )(emb, exps, in_hbm(scale), denom, chosen)


ITEMS = 2


def weight_kernel(joined, cols, p, q, op, oq, d, od, *refs):
    del cols
    step = pl.program_id(0)
    held, grads, extra, out_sems, in_sems = refs[-5:]
    outs = refs[-6:-5] if joined else refs[-5 - ITEMS : -5]
    added = refs[: len(refs) - 5 - len(outs)]
    tile = held.shape[1]
    rows = p.shape[0]
    states = (p, q, op, oq)
    copies = []
    for i, source in enumerate((d, od)):
        for j in range(2):
            number = len(copies)
            copies.append(
                pltpu.make_async_copy(
                    source.at[pl.ds(j * rows, rows), :], grads.at[number], in_sems.at[number]
                )
            )
    for i, source in enumerate(added):
        copies.append(
            pltpu.make_async_copy(source, extra.at[i], in_sems.at[len(states) + i])
        )
    sent = [
        pltpu.make_async_copy(
            held.at[i],
            outs[0].at[pl.ds(i * tile, tile), :] if joined else outs[i],
            out_sems.at[i],
        )
        for i in range(ITEMS)
    ]
    first_step = step == 0

    @pl.when(first_step)
    def _():
        for copy in copies:
            copy.start()

    value = None
    for i, state in enumerate(states):

        @pl.when(first_step)
        def _():
            copies[i].wait()

        term = dot(state[...], grads[i], (0, 0))
        value = term if value is None else value + term
    for i in range(ITEMS):

        @pl.when(step == i)
        def _():
            total = value
            if added:
                copies[len(states) + i].wait()
                total = value + extra[i].astype(F32)
            held[i] = total.astype(BF16)
            sent[i].start()

    @pl.when(step == ITEMS - 1)
    def _():
        for copy in sent:
            copy.wait()


def weight_terms(states, d_mine, d_other, u, items, part, added=(), joined=False):
    rows = states[0].shape[0]
    tile = part // 2
    keep = d_mine.shape[1]
    count = len(items)
    cols = jnp.stack([lax.rem(u + step, SIDE) * 2 + half for step, half in items])
    state = pl.BlockSpec((rows, tile), lambda i, cols: (0, cols[i]))
    anywhere = pl.BlockSpec(memory_space=pl.ANY)
    shapes = [(count * tile, keep)] if joined else [(tile, keep)] * count
    return pl.pallas_call(
        functools.partial(weight_kernel, joined),
        grid_spec=pltpu.PrefetchScalarGridSpec(
            num_scalar_prefetch=1,
            grid=(count,),
            in_specs=[state] * 4 + [anywhere] * (2 + len(added)),
            out_specs=[anywhere] * len(shapes),
            scratch_shapes=[
                pltpu.VMEM((count, tile, keep), BF16),
                pltpu.VMEM((4, rows, keep), BF16),
                pltpu.VMEM((max(1, len(added)), tile, keep), BF16),
                pltpu.SemaphoreType.DMA((count,)),
                pltpu.SemaphoreType.DMA((4 + count,)),
            ],
        ),
        out_shape=[jax.ShapeDtypeStruct(shape, BF16) for shape in shapes],
        compiler_params=limit(20),
        cost_estimate=cost(
            2 * rows * tile * keep * count, (2 * rows * tile + tile * keep) * count
        ),
        name="weight_terms",
    )(cols.astype(jnp.int32), *states, d_mine, d_other, *added)


def place_kernel(places, *refs):
    *pieces, out = refs
    count = len(pieces) // 2
    half = pieces[0].shape[1]
    rows = out.shape[0] // (SIDE * SIDE)
    core = places[2]
    for side in range(2):
        a = places[side]
        b = places[1 - side]

        def fill(column, side=side, a=a, b=b):
            for number in range(count):
                ref = pieces[side * count + number]
                for inner in range(ref.shape[0] // rows):
                    far = (0, 1, 2, 2, 3)[number]
                    rel = inner + (2 if number == 3 else 0)
                    row = lax.rem(a + far, SIDE) * SIDE + lax.rem(b + rel, SIDE)
                    out[pl.ds(pl.multiple_of(row * rows, rows), rows), column * half : (column + 1) * half] = (
                        ref[inner * rows : (inner + 1) * rows, :]
                    )

        @pl.when(core == 0)
        def _():
            fill(side)

        @pl.when(core != 0)
        def _():
            fill(1 - side)


def place_all(mine, other, u, v, core):
    total = SIDE * SIDE * (mine[0].shape[0] // SIDE)
    half = mine[0].shape[1]
    places = jnp.stack([u, v, core]).astype(jnp.int32)
    return pl.pallas_call(
        place_kernel,
        in_specs=[pl.BlockSpec(memory_space=pltpu.SMEM)] + [pl.BlockSpec(memory_space=pltpu.VMEM)] * 10,
        out_specs=pl.BlockSpec(memory_space=pltpu.VMEM),
        out_shape=jax.ShapeDtypeStruct((total, 2 * half), BF16),
        compiler_params=limit(10),
        name="place_all",
    )(places, *mine, *other)


def add(*values):
    total = values[0].astype(F32)
    for value in values[1:]:
        total = total + value.astype(F32)
    return total.astype(BF16)


def lines_of(mine, per_block):
    blocks, _ = mine.shape
    same = (mine[:, :, None, None] == mine[None, None, :, :]).astype(jnp.int32)
    before = (
        lax.broadcasted_iota(jnp.int32, (blocks, blocks), 1)
        < lax.broadcasted_iota(jnp.int32, (blocks, blocks), 0)
    ).astype(jnp.int32)
    place = jnp.sum(same * before[:, None, :, None], axis=(2, 3))
    return jnp.repeat((mine * CAP + place).T, per_block, axis=1)


def route_kernel(per_block, lines, states, facts, lead_facts, out):
    tile = out.shape[0]
    queries, depth = states.shape
    row = lax.broadcasted_iota(jnp.int32, (tile, queries), 0) + pl.program_id(0) * tile
    col = lax.broadcasted_iota(jnp.int32, (tile, queries), 1)
    aligned = jnp.bitwise_and(row, per_block - 1) == jnp.bitwise_and(col, per_block - 1)
    line = jnp.right_shift(row, per_block.bit_length() - 1)
    lead = aligned & (line == lines[0:1, :])
    both = lead | (aligned & (line == lines[1:2, :]))
    lead = jnp.where(lead, 1.0, 0.0).astype(BF16)
    both = jnp.where(both, 1.0, 0.0).astype(BF16)
    out[:, :depth] = dot(both, states[...], (1, 0)).astype(BF16)
    out[:, depth:] = (
        dot(both, facts[...], (1, 0)) + dot(lead, lead_facts[...], (1, 0))
    ).astype(BF16)


def route(lines, states, facts, lead_facts, rows, per_block):
    queries, depth = states.shape
    steps = 4
    wide = depth + facts.shape[1]

    def whole(value):
        return pl.BlockSpec(value.shape, lambda i: (0, 0))

    return pl.pallas_call(
        functools.partial(route_kernel, per_block),
        grid=(steps,),
        in_specs=[whole(value) for value in (lines, states, facts, lead_facts)],
        out_specs=pl.BlockSpec((rows // steps, wide), lambda i: (i, 0)),
        out_shape=pltpu.HBM((rows, wide), BF16),
        compiler_params=limit(10),
        cost_estimate=cost(2 * rows * queries * wide, 2 * (rows + queries) * wide),
        name="route",
    )(lines, states, facts, lead_facts)


def shards(query_states, passage_last_states, head_weight, negatives, positives):
    ranks = lax.axis_size("dp")
    groups = lax.axis_size("psg")
    dp = lax.axis_index("dp")
    column = lax.axis_index("psg")
    core = lax.rem(dp, 2)
    x = dp // (2 * SIDE)
    y = lax.rem(dp // 2, SIDE)
    u = jnp.where(core == 0, x, y)
    v = jnp.where(core == 0, y, x)
    queries, depth = query_states.shape
    blocks = negatives.shape[1]
    per_block = queries // blocks
    share = head_weight.shape[1]
    half = share // 2
    deep = depth // 2

    def own(row):
        return lax.dynamic_slice(head_weight, (row * deep, core * half), (deep, half))

    top, bottom, query_states = lax.optimization_barrier((own(0), own(1), query_states))
    left_top = third(top, 1)
    right_bottom = third(bottom, -1)
    left_bottom = third(bottom, 1)
    right_top = third(top, -1)
    sides = jnp.stack([core, 1 - core]).astype(jnp.int32)
    (raw_p0,) = project([passage_last_states], [head_weight], sides, 12)
    left_top, left_bottom, right_top, right_bottom, raw_p0 = lax.optimization_barrier(
        (left_top, left_bottom, right_top, right_bottom, raw_p0)
    )
    mine1 = [right_top, right_bottom]
    mine3 = [left_top, left_bottom]
    theirs1 = [swap(piece) for piece in mine1]
    theirs3 = [swap(piece) for piece in mine3]
    mine2 = [third(left_top, 1), third(right_bottom, -1)]

    picked = lax.dynamic_index_in_dim(negatives, column, 0, keepdims=False)
    lines = lines_of(picked, per_block)
    number = lax.broadcasted_iota(jnp.int32, (queries, 1), 0) // per_block
    facts = jnp.concatenate(
        [jnp.ones_like(number), number, positives[:, None] // 16, positives[:, None] % 16], axis=1
    ).astype(BF16)
    facts = jnp.pad(facts, ((0, 0), (0, 128 - facts.shape[1])))
    lead_facts = (
        (lax.broadcasted_iota(jnp.int32, facts.shape, 1) == 4) & (column == 0)
    ).astype(BF16)
    rows = ranks * CAP * per_block
    outgoing = route(lines, query_states, facts, lead_facts, rows, per_block)
    asked = lax.all_to_all(
        outgoing.reshape(ranks, rows // ranks, depth + 128),
        "dp",
        split_axis=0,
        concat_axis=0,
        tiled=True,
    ).reshape(rows, depth + 128)
    facts = asked[:, depth : depth + 8].astype(jnp.int32).T
    valid = facts[0:1]
    block_of = facts[1]
    chosen = jnp.where(facts[4:5] == 1, facts[2:3] * 16 + facts[3:4], -1)

    other_states = swap(passage_last_states)
    other_asked = swap(asked)

    near = [[mine1, theirs1], [mine3, theirs3]]
    raw_p1, raw_p3 = project([passage_last_states], near, sides, 17, COVER)
    asked, raw_p0, raw_p1, raw_p3 = lax.optimization_barrier((asked, raw_p0, raw_p1, raw_p3))
    raw_q0, raw_q1, raw_q3 = project([asked], [head_weight, *near], sides, 22)
    *mine2, raw_q0, raw_q1, raw_q3 = lax.optimization_barrier((*mine2, raw_q0, raw_q1, raw_q3))
    theirs2 = [swap(piece) for piece in mine2]
    raw_p2, raw_q2 = project([passage_last_states, asked], [[mine2, theirs2]], sides, 17, kept=True)
    emb, exps, scale, sums, hits = score(
        (raw_p0, raw_p1, raw_p2, raw_p3), (raw_q0, raw_q1, raw_q2, raw_q3), chosen, valid
    )

    spread = (
        block_of.reshape(ranks, CAP, 1, per_block)
        == lax.broadcasted_iota(jnp.int32, (1, 1, blocks, 1), 2)
    ).astype(F32)
    both = jnp.concatenate([sums, hits], axis=0).reshape(2, ranks, CAP, 1, per_block)
    both = jnp.sum(both * spread[None], axis=2)
    packed = both.reshape(-1, blocks * per_block)
    packed = ring_sum(packed, first)
    packed = ring_sum(packed, second)
    packed = packed + swap(packed)
    packed = ring_sum(packed, third)
    both = packed.reshape(2, ranks, blocks, per_block)
    losses = (jnp.log(both[0]) - both[1]).reshape(-1)
    out_share = queries // groups
    loss_out = lax.dynamic_slice_in_dim(losses, (dp * groups + column) * out_share, out_share, 0)
    denom = jnp.sum(both[0][:, None] * spread, axis=2).reshape(1, rows)
    denom = jnp.where(valid == 1, denom, 1.0)
    d_mine, d_theirs = backward(emb, exps, scale, denom, chosen)

    d_other = swap(d_theirs)
    states = (passage_last_states, asked, other_states, other_asked)
    part = depth // SIDE
    terms = functools.partial(weight_terms, states, d_mine, d_other, u, part=part)
    far0, far1 = terms(items=[(2, 0), (2, 1)])
    from_left = first(far0, 1)
    from_right = first(far1, -1)
    right1, left0 = terms(items=[(1, 1), (3, 0)])
    left1_in = first(right1, 1)
    right0_in = first(left0, -1)
    right0, left1 = terms(items=[(1, 0), (3, 1)], added=(from_left, from_right))
    left0_in = first(right0, 1)
    right1_in = first(left1, -1)
    (summed,) = terms(items=[(0, 0), (0, 1)], added=(right0_in, left1_in), joined=True)
    summed = add(summed, jnp.concatenate([left0_in, right1_in], axis=0))

    part2 = part // SIDE

    def chunk(step):
        return lax.dynamic_slice_in_dim(summed, lax.rem(v + step, SIDE) * part2, part2, 0)

    summed = add(
        chunk(0), second(chunk(1), 1), second(chunk(3), -1), second(chunk(2), 2)
    )
    cols = [summed[:, step * half : (step + 1) * half] for step in range(SIDE)]
    piece = add(cols[0], third(cols[1], 1), third(cols[3], -1), third(cols[2], 2))

    piece = jnp.concatenate(
        [piece, second(piece, -1), second(piece, 2), second(piece, 1)], axis=0
    )
    middle = piece.shape[0] // 2
    left = first(piece, 1)
    right = first(piece, -1)
    mine = [piece, right, first(left[:middle], 1), first(right[middle:], -1), left]
    other = [swap(block) for block in mine]
    return (loss_out, place_all(mine, other, u, v, core))


def solution(mesh):
    return jax.shard_map(
        shards,
        mesh=mesh,
        in_specs=(
            P("dp", None),
            P(("dp", "psg"), None),
            P(None, "psg"),
            P(None, "dp", None),
            P("dp"),
        ),
        out_specs=(P(("dp", "psg")), P(None, "psg")),
        check_vma=False,
    )
```
